256 devices in a mesh: gx: 32 (over y, z), gy: 8 (over x, core).
Axes of the slice: x: 4, y: 4, z: 8, core: 2. Of those that a mesh axis runs over, the one named last changes fastest.
Arguments:
- snapshot: float32 [1, 512, 128, 512], P(None, 'gx', 'gy'), may hold values from -25 to 25
Outputs:
- codes: float32 [1, 512, 128, 512], P(None, 'gx', 'gy')
The draws below stay inside these ranges and needn't reach their ends.
All inputs are finite; a program needn't handle non-finite values.
Results may differ from the reference program's by a relative error of at most 0.0003.
Values sent between devices are 32-bit elements; how exact they have to be, the bound alone decides.
No kernel may reach another device: no remote copies, remote signals or barrier semaphores. Data moves between devices by JAX's collectives and lax.ppermute only.
A program may use at most 64 MiB of HBM per device.

```python
import math
import jax
import jax.numpy as jnp
from jax import lax

F = 1
LEVELS = 2
NX = 512
NY = 128
NZ = 512


def draw_snapshot(key, part):
    key = jax.random.fold_in(key, 11)
    full_shape = (F, NX, NY, NZ)
    fluctuation = jax.random.truncated_normal(key, -4.0, 4.0, full_shape, jnp.float32)
    field_index = lax.broadcasted_iota(jnp.float32, full_shape, 0)
    x_position = lax.broadcasted_iota(jnp.float32, full_shape, 1)
    ramp_factor = 1.0 + 2.0 * x_position / (NX - 1)
    return ramp_factor * (0.5 + 0.3 * field_index) * fluctuation + 0.8 * jnp.cos(field_index)


def setup_inputs(seed: int = 0) -> dict:
    seeds = jax.random.split(jax.random.key(seed), 2)
    snapshot = draw_snapshot(jax.random.fold_in(seeds[1], 71), 0)
    return dict(snapshot=snapshot)


REL_BOUND = 0.01
TWO_PI = 2.0 * math.pi


def cubic(outer_low, inner_low, inner_high, outer_high):
    return (9.0 * (inner_low + inner_high) - (outer_low + outer_high)) / 16.0


def quantize(values, predicted, error_bound):
    scaled = (values - predicted) / (2.0 * error_bound)
    code_vals = scaled - jnp.sin(TWO_PI * scaled) / TWO_PI
    return code_vals, predicted + (2.0 * error_bound) * code_vals


def view_index(direction, stride, leading):
    source = [slice(None)] * leading
    target = [slice(None)] * leading
    for spatial in range(3):
        if spatial < direction:
            source.append(slice(0, None, stride))
            target.append(slice(0, None, stride))
        elif spatial == direction:
            source.append(slice(0, None, 2 * stride))
            target.append(slice(stride, None, 2 * stride))
        else:
            source.append(slice(0, None, 2 * stride))
            target.append(slice(0, None, 2 * stride))
    return tuple(source), tuple(target)


def compress_field(field, error_bound):
    rebuilt = field
    code_grid = jnp.zeros_like(field)
    for depth_level in range(LEVELS, 0, -1):
        stride = 2 ** (depth_level - 1)
        for direction in range(3):
            source_index, target_index = view_index(direction, stride, 0)
            known = rebuilt[source_index]
            predicted = cubic(jnp.roll(known, 1, direction), known,
                              jnp.roll(known, -1, direction), jnp.roll(known, -2, direction))
            new_codes, new_values = quantize(field[target_index], predicted, error_bound)
            rebuilt = rebuilt.at[target_index].set(new_values)
            code_grid = code_grid.at[target_index].set(new_codes)
    return code_grid


def reference(snapshot):
    outputs = []
    for ordinal in range(F):
        field = snapshot[ordinal]
        error_bound = REL_BOUND * (jnp.max(field) - jnp.min(field))
        outputs.append(compress_field(field, error_bound))
    return jnp.stack(outputs, axis=0)
```

```python
import math

import jax
import jax.numpy as jnp
from jax import lax
from jax.experimental import pallas as pl
from jax.experimental.pallas import tpu as pltpu
from jax.sharding import PartitionSpec as P

REL_BOUND = 0.01
AXES = ("gx", "gy")

Q_COEFFS = (6.579714775085449, -12.986868858337402, 12.191614151000977, -6.570947170257568, 1.9706368446350098)

PLANES = 33
ROWS = 24
OWN_X = 8
OWN_R = 8
PAIRS = 8

LOW_X = (8, 12, 14)
HIGH_X = (0, 2, 4, 8)
LOW_TILES = ((0, 8), (0, 12), (0, 14), (1, 14))
HIGH_TILES = ((0, 0), (0, 2), (1, 0), (1, 2), (0, 4), (0, 8))


def lane_index():
    return lax.broadcasted_iota(jnp.int32, (8, 128), 1)


def swap_stage(first, second, keep, width):
    merged = jnp.where(keep, first, pltpu.roll(second, width, 1))
    other = jnp.where(keep, pltpu.roll(first, 128 - width, 1), second)
    return merged, other


def block_transpose(parts, lane):
    low_half = lane < 64
    low_quarter = (lane % 64) < 32
    a0, a2 = swap_stage(parts[0], parts[2], low_half, 64)
    a1, a3 = swap_stage(parts[1], parts[3], low_half, 64)
    b0, b1 = swap_stage(a0, a1, low_quarter, 32)
    b2, b3 = swap_stage(a2, a3, low_quarter, 32)
    return b0, b1, b2, b3


def split_phases(chunks, lane):
    order = 4 * (lane % 32) + lane // 32
    sorted_chunks = [jnp.take_along_axis(c, order, axis=1) for c in chunks]
    return block_transpose(sorted_chunks, lane)


def merge_phases(phases, lane):
    order = 32 * (lane % 4) + lane // 4
    blocks = block_transpose(phases, lane)
    return [jnp.take_along_axis(b, order, axis=1) for b in blocks]


def prepare_kernel(block_ref, even_ref, odd_ref, rest_ref, low_ref, high_ref, peak_ref, scratch):
    lane = lane_index()
    highest = None
    lowest = None
    for x in range(16):
        for t in range(2):
            chunks = [block_ref[x, 8 * t : 8 * t + 8, 128 * k : 128 * k + 128] for k in range(4)]
            top = jnp.maximum(jnp.maximum(chunks[0], chunks[1]), jnp.maximum(chunks[2], chunks[3]))
            low = jnp.minimum(jnp.minimum(chunks[0], chunks[1]), jnp.minimum(chunks[2], chunks[3]))
            highest = top if highest is None else jnp.maximum(highest, top)
            lowest = low if lowest is None else jnp.minimum(lowest, low)
            phases = split_phases(chunks, lane)
            rest_ref[0, x, 8 * t : 8 * t + 8, :] = phases[1]
            rest_ref[1, x, 8 * t : 8 * t + 8, :] = phases[3]
            scratch[0, x, 8 * t : 8 * t + 8, :] = phases[0]
            scratch[1, x, 8 * t : 8 * t + 8, :] = phases[2]
    for x in range(16):
        for z in range(2):
            even_ref[z, x] = scratch[z, x, pl.ds(0, 8, stride=2), :]
            odd_ref[z, x] = scratch[z, x, pl.ds(1, 8, stride=2), :]
    for i, (z, x) in enumerate(LOW_TILES):
        low_ref[i] = even_ref[z, x]
    for i, (z, x) in enumerate(HIGH_TILES):
        high_ref[i] = even_ref[z, x]
    peak = jnp.where(lax.broadcasted_iota(jnp.int32, (1, 128), 1) < 64, jnp.max(highest), -jnp.min(lowest))
    peak_ref[...] = jnp.broadcast_to(peak, peak_ref.shape)


def code_of(scaled):
    whole = jnp.round(scaled)
    r = scaled - whole
    s = r * r
    q = Q_COEFFS[-1]
    for c in Q_COEFFS[-2::-1]:
        q = q * s + c
    return whole + (r * s) * q


def compress_kernel(
    even_ref, odd_ref, rest_ref, ylow_ref, yhigh_ref, xlow_ref, xhigh_ref, ll_ref, lh_ref, hl_ref, hh_ref,
    peaks_ref, out_ref, known0, known2, codes0, codes2, full0, full2, fullc0, fullc2,
):
    lane = lane_index()
    known = (known0, known2)
    codes = (codes0, codes2)
    full = (full0, full2)
    fullc = (fullc0, fullc2)

    def plane(x):
        return (x + OWN_X) * ROWS

    for z in range(2):
        for x in range(16):
            base = plane(x)
            known[z][base : base + 8, :] = ylow_ref[z, x]
            known[z][base + 8 : base + 16, :] = even_ref[z, x]
            known[z][base + 16 : base + 24, :] = yhigh_ref[z, x]
    for i, (z, x) in enumerate(LOW_TILES):
        base = plane(x - 16)
        known[z][base : base + 8, :] = ll_ref[i]
        known[z][base + 8 : base + 16, :] = xlow_ref[i]
        known[z][base + 16 : base + 24, :] = lh_ref[i]
    for i, (z, x) in enumerate(HIGH_TILES):
        base = plane(x + 16)
        known[z][base : base + 8, :] = hl_ref[i]
        known[z][base + 8 : base + 16, :] = xhigh_ref[i]
        known[z][base + 16 : base + 24, :] = hh_ref[i]

    peaks = peaks_ref[0:8, :]
    for i in range(1, peaks_ref.shape[0] // 8):
        peaks = jnp.maximum(peaks, peaks_ref[8 * i : 8 * i + 8, :])
    upper = jnp.max(jnp.where(lane < 64, peaks, -jnp.inf))
    lower = jnp.max(jnp.where(lane < 64, -jnp.inf, peaks))
    step = jnp.full((1, 1), 2.0 * (REL_BOUND * (upper + lower)), jnp.float32)
    inverse = 1.0 / step

    def quantize(values, outer_low, inner_low, inner_high, outer_high):
        predicted = 0.5625 * (inner_low + inner_high) - 0.0625 * (outer_low + outer_high)
        code = code_of((values - predicted) * inverse)
        return code, predicted + step * code

    for x in range(-2, 19, 4):
        rows = [plane(x + d) + OWN_R - 4 for d in (0, -6, -2, 2, 6)]
        args = [known0[pl.ds(r, 8, stride=2), :] for r in rows]
        code, value = quantize(*args)
        known0[pl.ds(rows[0], 8, stride=2), :] = value
        codes0[pl.ds(rows[0], 8, stride=2), :] = code
    rows = [plane(-2 + d) + OWN_R + 12 for d in (0, -6, -2, 2, 6)]
    args = [known0[pl.ds(r, 6, stride=4 * ROWS), :] for r in rows]
    code, value = quantize(*args)
    known0[pl.ds(rows[0], 6, stride=4 * ROWS), :] = value

    for x in range(-2, 19, 2):
        first = plane(x) + OWN_R - 1
        args = [known0[pl.ds(first + d, 6, stride=2), :] for d in (0, -3, -1, 1, 3)]
        code, value = quantize(*args)
        known0[pl.ds(first, 6, stride=2), :] = value
        codes0[pl.ds(first, 6, stride=2), :] = code

    for x in range(-2, 19, 2):
        for first, count in ((OWN_R - 1, 8), (OWN_R + 7, 3)):
            rows = pl.ds(plane(x) + first, count)
            k = known0[rows, :]
            code, value = quantize(
                known2[rows, :], pltpu.roll(k, 1, 1), k, pltpu.roll(k, 127, 1), pltpu.roll(k, 126, 1)
            )
            known2[rows, :] = value
            codes2[rows, :] = code
    for x in range(0, 16, 4):
        codes0[pl.ds(plane(x) + OWN_R, 4, stride=2), :] = jnp.zeros((4, 128), jnp.float32)

    for x in range(1, 16, 2):
        for first, count in ((OWN_R - 1, 8), (OWN_R + 7, 3)):
            for z in range(2):
                args = [known[z][pl.ds(plane(x + d) + first, count), :] for d in (0, -3, -1, 1, 3)]
                code, value = quantize(*args)
                known[z][pl.ds(plane(x) + first, count), :] = value
                codes[z][pl.ds(plane(x) + first, count), :] = code

    for x in range(16):
        for z in range(2):
            base = plane(x) + OWN_R
            inner = known[z][pl.ds(base, 8), :]
            code, value = quantize(
                odd_ref[z, x],
                known[z][pl.ds(base - 1, 8), :],
                inner,
                known[z][pl.ds(base + 1, 8), :],
                known[z][pl.ds(base + 2, 8), :],
            )
            full[z][x, pl.ds(0, 8, stride=2), :] = inner
            full[z][x, pl.ds(1, 8, stride=2), :] = value
            fullc[z][x, pl.ds(0, 8, stride=2), :] = codes[z][pl.ds(base, 8), :]
            fullc[z][x, pl.ds(1, 8, stride=2), :] = code
        for t in range(2):
            rows = slice(8 * t, 8 * t + 8)
            k0 = full0[x, rows, :]
            k2 = full2[x, rows, :]
            k0_next = pltpu.roll(k0, 127, 1)
            k2_next = pltpu.roll(k2, 127, 1)
            k2_last = pltpu.roll(k2, 1, 1)
            code1, _ = quantize(rest_ref[0, x, rows, :], k2_last, k0, k2, k0_next)
            code3, _ = quantize(rest_ref[1, x, rows, :], k0, k2, k0_next, k2_next)
            merged = merge_phases([fullc0[x, rows, :], code1, fullc2[x, rows, :], code3], lane)
            for k in range(4):
                out_ref[x, rows, 128 * k : 128 * k + 128] = merged[k]


def shards(snapshot):
    nx = lax.axis_size("gx")
    ny = lax.axis_size("gy")
    f32 = jnp.float32
    vmem = pl.BlockSpec(memory_space=pltpu.VMEM)
    block = snapshot.reshape(snapshot.shape[1:])
    shape = jax.ShapeDtypeStruct
    even, odd, rest, low, high, peak = pl.pallas_call(
        prepare_kernel,
        in_specs=[vmem],
        out_specs=[vmem] * 6,
        out_shape=[
            shape((2, 16, 8, 128), f32),
            shape((2, 16, 8, 128), f32),
            shape((2, 16, 16, 128), f32),
            shape((len(LOW_TILES), 8, 128), f32),
            shape((len(HIGH_TILES), 8, 128), f32),
            shape((nx * ny, 128), f32),
        ],
        scratch_shapes=[pltpu.VMEM((2, 16, 16, 128), f32)],
        compiler_params=pltpu.CompilerParams(vmem_limit_bytes=16 * 1024 * 1024),
        name="prepare",
    )(block)

    def shifted(array, dx, dy):
        pairs = []
        for x in range(nx):
            for y in range(ny):
                pairs.append((x * ny + y, (x + dx) % nx * ny + (y + dy) % ny))
        return lax.ppermute(array, AXES, pairs)

    ylow = shifted(even, 0, 1)
    yhigh = shifted(even, 0, -1)
    xlow = shifted(low, 1, 0)
    xhigh = shifted(high, -1, 0)
    ll = shifted(low, 1, 1)
    lh = shifted(low, 1, -1)
    hl = shifted(high, -1, 1)
    hh = shifted(high, -1, -1)
    peaks = lax.all_to_all(peak, AXES, 0, 0, tiled=True)

    codes = pl.pallas_call(
        compress_kernel,
        in_specs=[vmem] * 12,
        out_specs=vmem,
        out_shape=shape(block.shape, f32),
        scratch_shapes=[pltpu.VMEM((PLANES * ROWS, 128), f32)] * 4 + [pltpu.VMEM((16, 16, 128), f32)] * 4,
        compiler_params=pltpu.CompilerParams(vmem_limit_bytes=24 * 1024 * 1024),
        name="compress",
    )(even, odd, rest, ylow, yhigh, xlow, xhigh, ll, lh, hl, hh, peaks)
    return codes.reshape(snapshot.shape)


def solution(mesh):
    spec = P(None, "gx", "gy", None)
    return jax.shard_map(shards, mesh=mesh, in_specs=(spec,), out_specs=spec, check_vma=False)
```

```python
import jax
import jax.numpy as jnp
from jax import lax
from jax.experimental import pallas as pl
from jax.experimental.pallas import tpu as pltpu
from jax.sharding import PartitionSpec as P

REL_BOUND = 0.01
AXES = ("gx", "gy")

Q_COEFFS = (6.579714775085449, -12.986868858337402, 12.191614151000977, -6.570947170257568, 1.9706368446350098)

PLANES = 33
ROWS = 24
OWN_X = 8
OWN_R = 8

LOW_PLANES = ((0, 8), (0, 12), (0, 14), (1, 14))
HIGH_PLANES = ((0, 0), (0, 2), (1, 0), (1, 2), (0, 4), (0, 8))
LOW_ROWS = ((0, 14, 1), (1, 14, 1), (0, 8, 2), (0, 12, 2))
HIGH_ROWS = ((0, 0, 1), (1, 0, 1), (0, 2, 1), (1, 2, 1), (0, 4, 2), (0, 8, 2))
F32 = jnp.float32
BF16 = jnp.bfloat16


def packed_at(rows):
    at, places = 0, []
    for _, _, step in rows:
        places.append(at)
        at += 16 // step
    return places, at


LOW_AT, LOW_COUNT = packed_at(LOW_ROWS)
HIGH_AT, HIGH_COUNT = packed_at(HIGH_ROWS)


def permute_lanes(values, matrix):
    first = values.astype(BF16)
    rest = values - first.astype(F32)
    second = rest.astype(BF16)
    third = (rest - second.astype(F32)).astype(BF16)
    parts = [jnp.dot(piece, matrix, preferred_element_type=F32) for piece in (first, second, third)]
    return parts[0] + (parts[1] + parts[2])


def prepare_kernel(block_ref, phase_ref, low_ref, high_ref, peak_ref):
    highest = [None] * 4
    lowest = [None] * 4
    for x in range(16):
        for t in range(2):
            for k in range(4):
                chunk = block_ref[x, 8 * t : 8 * t + 8, 128 * k : 128 * k + 128]
                highest[k] = chunk if highest[k] is None else jnp.maximum(highest[k], chunk)
                lowest[k] = chunk if lowest[k] is None else jnp.minimum(lowest[k], chunk)
    upper = jnp.maximum(jnp.maximum(highest[0], highest[1]), jnp.maximum(highest[2], highest[3]))
    lower = -jnp.minimum(jnp.minimum(lowest[0], lowest[1]), jnp.minimum(lowest[2], lowest[3]))
    lane = lax.broadcasted_iota(jnp.int32, (8, 128), 1)
    upper = jnp.maximum(upper, pltpu.roll(upper, 64, 1))
    lower = jnp.maximum(lower, pltpu.roll(lower, 64, 1))
    peak = jnp.where(lane < 64, upper, lower)
    for s in (4, 2, 1):
        peak = jnp.maximum(peak, pltpu.roll(peak, s, 0))
    for i in range(peak_ref.shape[0] // 8):
        peak_ref[8 * i : 8 * i + 8, :] = peak

    source = lax.broadcasted_iota(jnp.int32, (256, 256), 0)
    target = lax.broadcasted_iota(jnp.int32, (256, 256), 1)
    matrix = (source == 4 * (target % 64) + target // 64).astype(F32).astype(BF16)
    halves = [permute_lanes(block_ref[:, :, 256 * h : 256 * h + 256].reshape(256, 256), matrix) for h in range(2)]
    low_half = lax.broadcasted_iota(jnp.int32, (256, 128), 1) < 64
    for j in range(2):
        a = halves[0][:, 128 * j : 128 * j + 128]
        b = halves[1][:, 128 * j : 128 * j + 128]
        phase_ref[2 * j] = jnp.where(low_half, a, pltpu.roll(b, 64, 1))
        phase_ref[2 * j + 1] = jnp.where(low_half, pltpu.roll(a, 64, 1), b)

    for ref, rows, places in ((low_ref, LOW_ROWS, LOW_AT), (high_ref, HIGH_ROWS, HIGH_AT)):
        for (z, y, step), at in zip(rows, places):
            for half in range(2 // step):
                ref[at + 8 * half : at + 8 * half + 8, :] = phase_ref[
                    2 * z, pl.ds(16 * 8 * half + y, 8, stride=16 * step), :
                ]


def join_kernel(phase_ref, ylow_ref, yhigh_ref, low_ref, high_ref):
    for ref, planes in ((low_ref, LOW_PLANES), (high_ref, HIGH_PLANES)):
        for i, (z, x) in enumerate(planes):
            base = ROWS * i
            ref[base + OWN_R : base + OWN_R + 8, :] = phase_ref[2 * z, pl.ds(16 * x, 8, stride=2), :]
            for source, rows, places, shift in ((ylow_ref, LOW_ROWS, LOW_AT, -16), (yhigh_ref, HIGH_ROWS, HIGH_AT, 16)):
                for (zz, y, step), at in zip(rows, places):
                    if zz == z and x % step == 0:
                        r = base + OWN_R + (y + shift) // 2
                        ref[r : r + 1, :] = source[at + x // step : at + x // step + 1, :]


def code_of(scaled):
    whole = jnp.round(scaled)
    r = scaled - whole
    s = r * r
    q = Q_COEFFS[-1]
    for c in Q_COEFFS[-2::-1]:
        q = q * s + c
    return whole + (r * s) * q


def compress_kernel(
    phase_ref, ylow_ref, yhigh_ref, xlow_ref, xhigh_ref, peaks_ref, out_ref,
    known0, known2, codes0, codes2, full0, full2, fullc0, fullc1, fullc2, fullc3,
):
    lane = lax.broadcasted_iota(jnp.int32, (8, 128), 1)
    known = (known0, known2)
    codes = (codes0, codes2)
    full = (full0, full2)
    fullc = (fullc0, fullc2)

    def plane(x):
        return (x + OWN_X) * ROWS

    for z in range(2):
        for x in range(16):
            base = plane(x) + OWN_R
            known[z][base : base + 8, :] = phase_ref[2 * z, pl.ds(16 * x, 8, stride=2), :]
    for source, rows, places, shift in ((ylow_ref, LOW_ROWS, LOW_AT, -16), (yhigh_ref, HIGH_ROWS, HIGH_AT, 16)):
        for (z, y, step), at in zip(rows, places):
            r = plane(0) + OWN_R + (y + shift) // 2
            for half in range(2 // step):
                known[z][pl.ds(r + 8 * half * ROWS, 8, stride=step * ROWS), :] = source[at + 8 * half : at + 8 * half + 8, :]
    for source, planes, shift in ((xlow_ref, LOW_PLANES, -16), (xhigh_ref, HIGH_PLANES, 16)):
        for i, (z, x) in enumerate(planes):
            base = plane(x + shift)
            for t in range(3):
                known[z][base + 8 * t : base + 8 * t + 8, :] = source[ROWS * i + 8 * t : ROWS * i + 8 * t + 8, :]

    peaks = peaks_ref[0:8, :]
    for i in range(1, peaks_ref.shape[0] // 8):
        peaks = jnp.maximum(peaks, peaks_ref[8 * i : 8 * i + 8, :])
    upper = jnp.max(jnp.where(lane < 64, peaks, -jnp.inf))
    lower = jnp.max(jnp.where(lane < 64, -jnp.inf, peaks))
    step = jnp.full((1, 1), 2.0 * (REL_BOUND * (upper + lower)), F32)
    inverse = 1.0 / step

    def quantize(values, outer_low, inner_low, inner_high, outer_high):
        predicted = 0.5625 * (inner_low + inner_high) - 0.0625 * (outer_low + outer_high)
        code = code_of((values - predicted) * inverse)
        return code, predicted + step * code

    for x in range(-2, 19, 4):
        rows = [plane(x + d) + OWN_R - 4 for d in (0, -6, -2, 2, 6)]
        args = [known0[pl.ds(r, 8, stride=2), :] for r in rows]
        code, value = quantize(*args)
        known0[pl.ds(rows[0], 8, stride=2), :] = value
        codes0[pl.ds(rows[0], 8, stride=2), :] = code
    rows = [plane(-2 + d) + OWN_R + 12 for d in (0, -6, -2, 2, 6)]
    args = [known0[pl.ds(r, 6, stride=4 * ROWS), :] for r in rows]
    code, value = quantize(*args)
    known0[pl.ds(rows[0], 6, stride=4 * ROWS), :] = value

    for x in range(-2, 19, 2):
        first = plane(x) + OWN_R - 1
        args = [known0[pl.ds(first + d, 6, stride=2), :] for d in (0, -3, -1, 1, 3)]
        code, value = quantize(*args)
        known0[pl.ds(first, 6, stride=2), :] = value
        codes0[pl.ds(first, 6, stride=2), :] = code

    for x in range(-2, 19, 2):
        for first, count in ((OWN_R - 1, 8), (OWN_R + 7, 3)):
            rows = pl.ds(plane(x) + first, count)
            k = known0[rows, :]
            code, value = quantize(
                known2[rows, :], pltpu.roll(k, 1, 1), k, pltpu.roll(k, 127, 1), pltpu.roll(k, 126, 1)
            )
            known2[rows, :] = value
            codes2[rows, :] = code
    for x in range(0, 16, 4):
        codes0[pl.ds(plane(x) + OWN_R, 4, stride=2), :] = jnp.zeros((4, 128), F32)

    for x in range(1, 16, 2):
        for first, count in ((OWN_R - 1, 8), (OWN_R + 7, 3)):
            for z in range(2):
                args = [known[z][pl.ds(plane(x + d) + first, count), :] for d in (0, -3, -1, 1, 3)]
                code, value = quantize(*args)
                known[z][pl.ds(plane(x) + first, count), :] = value
                codes[z][pl.ds(plane(x) + first, count), :] = code

    for x in range(16):
        for z in range(2):
            base = plane(x) + OWN_R
            inner = known[z][pl.ds(base, 8), :]
            code, value = quantize(
                phase_ref[2 * z, pl.ds(16 * x + 1, 8, stride=2), :],
                known[z][pl.ds(base - 1, 8), :],
                inner,
                known[z][pl.ds(base + 1, 8), :],
                known[z][pl.ds(base + 2, 8), :],
            )
            full[z][pl.ds(16 * x, 8, stride=2), :] = inner
            full[z][pl.ds(16 * x + 1, 8, stride=2), :] = value
            fullc[z][pl.ds(16 * x, 8, stride=2), :] = codes[z][pl.ds(base, 8), :]
            fullc[z][pl.ds(16 * x + 1, 8, stride=2), :] = code
        for t in range(2):
            rows = slice(16 * x + 8 * t, 16 * x + 8 * t + 8)
            k0 = full0[rows, :]
            k2 = full2[rows, :]
            k0_next = pltpu.roll(k0, 127, 1)
            k2_next = pltpu.roll(k2, 127, 1)
            k2_last = pltpu.roll(k2, 1, 1)
            fullc1[rows, :], _ = quantize(phase_ref[1, rows, :], k2_last, k0, k2, k0_next)
            fullc3[rows, :], _ = quantize(phase_ref[3, rows, :], k0, k2, k0_next, k2_next)

    source = lax.broadcasted_iota(jnp.int32, (256, 256), 0)
    target = lax.broadcasted_iota(jnp.int32, (256, 256), 1)
    matrix = (target == 4 * (source % 64) + source // 64).astype(F32).astype(BF16)
    low_half = lax.broadcasted_iota(jnp.int32, (256, 128), 1) < 64
    parts = [fullc0[...], fullc1[...], fullc2[...], fullc3[...]]
    turned = [pltpu.roll(p, 64, 1) for p in parts]
    first = jnp.concatenate(
        [jnp.where(low_half, parts[0], turned[1]), jnp.where(low_half, parts[2], turned[3])], axis=1
    )
    second = jnp.concatenate(
        [jnp.where(low_half, turned[0], parts[1]), jnp.where(low_half, turned[2], parts[3])], axis=1
    )
    out_ref[:, :, 0:256] = permute_lanes(first, matrix).reshape(16, 16, 256)
    out_ref[:, :, 256:512] = permute_lanes(second, matrix).reshape(16, 16, 256)


def shards(snapshot):
    nx = lax.axis_size("gx")
    ny = lax.axis_size("gy")
    vmem = pl.BlockSpec(memory_space=pltpu.VMEM)
    block = snapshot.reshape(snapshot.shape[1:])
    params = pltpu.CompilerParams(vmem_limit_bytes=16 * 1024 * 1024)

    def shape(*dims):
        return jax.ShapeDtypeStruct(dims, F32)

    phases, low, high, peak = pl.pallas_call(
        prepare_kernel,
        in_specs=[vmem],
        out_specs=[vmem] * 4,
        out_shape=[shape(4, 256, 128), shape(LOW_COUNT, 128), shape(HIGH_COUNT, 128), shape(nx * ny, 128)],
        compiler_params=params,
        name="prepare",
    )(block)

    def shifted(array, axis, d):
        n = lax.axis_size(axis)
        return lax.ppermute(array, axis, [(i, (i + d) % n) for i in range(n)])

    peaks = lax.all_to_all(peak, AXES, 0, 0, tiled=True)
    ylow = shifted(low, "gy", 1)
    yhigh = shifted(high, "gy", -1)
    low_planes, high_planes = pl.pallas_call(
        join_kernel,
        in_specs=[vmem] * 3,
        out_specs=[vmem] * 2,
        out_shape=[shape(ROWS * len(LOW_PLANES), 128), shape(ROWS * len(HIGH_PLANES), 128)],
        compiler_params=params,
        cost_estimate=pl.CostEstimate(flops=2 * 10**10, bytes_accessed=10**6, transcendentals=0),
        name="join",
    )(phases, ylow, yhigh)
    xlow = shifted(low_planes, "gx", 1)
    xhigh = shifted(high_planes, "gx", -1)

    codes = pl.pallas_call(
        compress_kernel,
        in_specs=[vmem] * 6,
        out_specs=vmem,
        out_shape=shape(*block.shape),
        scratch_shapes=[pltpu.VMEM((PLANES * ROWS, 128), F32)] * 4 + [pltpu.VMEM((256, 128), F32)] * 6,
        compiler_params=params,
        name="compress",
    )(phases, ylow, yhigh, xlow, xhigh, peaks)
    return codes.reshape(snapshot.shape)


def solution(mesh):
    spec = P(None, "gx", "gy", None)
    return jax.shard_map(shards, mesh=mesh, in_specs=(spec,), out_specs=spec, check_vma=False)
```

```python
import jax
import jax.numpy as jnp
from jax import lax
from jax.experimental import pallas as pl
from jax.experimental.pallas import tpu as pltpu
from jax.sharding import PartitionSpec as P

REL_BOUND = 0.01
AXES = ("gx", "gy")

Q_COEFFS = (6.579714775085449, -12.986868858337402, 12.191614151000977, -6.570947170257568, 1.9706368446350098)

PLANES = 33
ROWS = 24
OWN_X = 8
OWN_R = 8

LOW_PLANES = ((0, 8), (0, 12), (0, 14), (1, 14))
HIGH_PLANES = ((0, 0), (0, 2), (1, 0), (1, 2), (0, 4), (0, 8))
LOW_ROWS = ((0, 14, 1), (1, 14, 1), (0, 8, 2), (0, 12, 2))
HIGH_ROWS = ((0, 0, 1), (1, 0, 1), (0, 2, 1), (1, 2, 1), (0, 4, 2), (0, 8, 2))
F32 = jnp.float32
BF16 = jnp.bfloat16


def packed_at(rows):
    at, places = 0, []
    for _, _, step in rows:
        places.append(at)
        at += 16 // step
    return places, at


LOW_AT, LOW_COUNT = packed_at(LOW_ROWS)
HIGH_AT, HIGH_COUNT = packed_at(HIGH_ROWS)


def plane_pieces(planes, total):
    main, extra = [], []
    for i, (z, x) in enumerate(planes):
        if z == 1:
            main.append((i, z, x, 7, 8, 1))
            extra.append((i, z, x, 15, 3, 1))
            continue
        if x in (0, 2, 14):
            main.append((i, z, x, 4, 8, 1))
            main.append((i, z, x, 12, 8, 1))
        else:
            main.append((i, z, x, 4, 8, 2))
        extra.append((i, z, x, 20, 1, 1))
    at, pieces = 0, []
    for piece in main + extra:
        pieces.append(piece + (at,))
        at += piece[4]
    assert at <= total
    return pieces


LOW_TOTAL = 88
HIGH_TOTAL = 80
LOW_PIECES = plane_pieces(LOW_PLANES, LOW_TOTAL)
HIGH_PIECES = plane_pieces(HIGH_PLANES, HIGH_TOTAL)


def row_slice(first, count, step):
    return pl.ds(first, count) if step == 1 else pl.ds(first, count, stride=step)


def permute_lanes(values, matrix):
    first = values.astype(BF16)
    rest = values - first.astype(F32)
    second = rest.astype(BF16)
    third = (rest - second.astype(F32)).astype(BF16)
    parts = [jnp.dot(piece, matrix, preferred_element_type=F32) for piece in (first, second, third)]
    return parts[0] + (parts[1] + parts[2])


def prepare_kernel(block_ref, phase_ref, low_ref, high_ref, peak_ref):
    highest = [None] * 4
    lowest = [None] * 4
    for x in range(16):
        for t in range(2):
            for k in range(4):
                chunk = block_ref[x, 8 * t : 8 * t + 8, 128 * k : 128 * k + 128]
                highest[k] = chunk if highest[k] is None else jnp.maximum(highest[k], chunk)
                lowest[k] = chunk if lowest[k] is None else jnp.minimum(lowest[k], chunk)
    upper = jnp.maximum(jnp.maximum(highest[0], highest[1]), jnp.maximum(highest[2], highest[3]))
    lower = -jnp.minimum(jnp.minimum(lowest[0], lowest[1]), jnp.minimum(lowest[2], lowest[3]))
    lane = lax.broadcasted_iota(jnp.int32, (8, 128), 1)
    upper = jnp.maximum(upper, pltpu.roll(upper, 64, 1))
    lower = jnp.maximum(lower, pltpu.roll(lower, 64, 1))
    peak = jnp.where(lane < 64, upper, lower)
    for s in (4, 2, 1):
        peak = jnp.maximum(peak, pltpu.roll(peak, s, 0))
    for i in range(peak_ref.shape[0] // 8):
        peak_ref[8 * i : 8 * i + 8, :] = peak

    source = lax.broadcasted_iota(jnp.int32, (256, 256), 0)
    target = lax.broadcasted_iota(jnp.int32, (256, 256), 1)
    matrix = (source == 4 * (target % 64) + target // 64).astype(F32).astype(BF16)
    halves = [permute_lanes(block_ref[:, :, 256 * h : 256 * h + 256].reshape(256, 256), matrix) for h in range(2)]
    low_half = lax.broadcasted_iota(jnp.int32, (256, 128), 1) < 64
    for j in range(2):
        a = halves[0][:, 128 * j : 128 * j + 128]
        b = halves[1][:, 128 * j : 128 * j + 128]
        phase_ref[2 * j] = jnp.where(low_half, a, pltpu.roll(b, 64, 1))
        phase_ref[2 * j + 1] = jnp.where(low_half, pltpu.roll(a, 64, 1), b)

    for ref, rows, places in ((low_ref, LOW_ROWS, LOW_AT), (high_ref, HIGH_ROWS, HIGH_AT)):
        for (z, y, step), at in zip(rows, places):
            for half in range(2 // step):
                ref[at + 8 * half : at + 8 * half + 8, :] = phase_ref[
                    2 * z, pl.ds(16 * 8 * half + y, 8, stride=16 * step), :
                ]


def join_kernel(phase_ref, ylow_ref, yhigh_ref, low_ref, high_ref, low_planes, high_planes):
    for ref, planes, out, pieces in (
        (low_planes, LOW_PLANES, low_ref, LOW_PIECES),
        (high_planes, HIGH_PLANES, high_ref, HIGH_PIECES),
    ):
        for i, (z, x) in enumerate(planes):
            base = ROWS * i
            ref[base + OWN_R : base + OWN_R + 8, :] = phase_ref[2 * z, pl.ds(16 * x, 8, stride=2), :]
            for source, rows, places, shift in ((ylow_ref, LOW_ROWS, LOW_AT, -16), (yhigh_ref, HIGH_ROWS, HIGH_AT, 16)):
                for (zz, y, step), at in zip(rows, places):
                    if zz == z and x % step == 0:
                        r = base + OWN_R + (y + shift) // 2
                        ref[r : r + 1, :] = source[at + x // step : at + x // step + 1, :]
        for i, z, x, first, count, step, at in pieces:
            out[at : at + count, :] = ref[row_slice(ROWS * i + first, count, step), :]


def code_of(scaled):
    whole = jnp.round(scaled)
    r = scaled - whole
    s = r * r
    q = Q_COEFFS[-1]
    for c in Q_COEFFS[-2::-1]:
        q = q * s + c
    return whole + (r * s) * q


def compress_kernel(
    phase_ref, ylow_ref, yhigh_ref, xlow_ref, xhigh_ref, peaks_ref, out_ref,
    known0, known2, codes0, codes2, full0, full2, fullc0, fullc1, fullc2, fullc3,
):
    lane = lax.broadcasted_iota(jnp.int32, (8, 128), 1)
    known = (known0, known2)
    codes = (codes0, codes2)
    full = (full0, full2)
    fullc = (fullc0, fullc2)

    def plane(x):
        return (x + OWN_X) * ROWS

    for z in range(2):
        for x in range(16):
            base = plane(x) + OWN_R
            known[z][base : base + 8, :] = phase_ref[2 * z, pl.ds(16 * x, 8, stride=2), :]
    for source, rows, places, shift in ((ylow_ref, LOW_ROWS, LOW_AT, -16), (yhigh_ref, HIGH_ROWS, HIGH_AT, 16)):
        for (z, y, step), at in zip(rows, places):
            r = plane(0) + OWN_R + (y + shift) // 2
            for half in range(2 // step):
                known[z][pl.ds(r + 8 * half * ROWS, 8, stride=step * ROWS), :] = source[at + 8 * half : at + 8 * half + 8, :]
    for source, pieces, shift in ((xlow_ref, LOW_PIECES, -16), (xhigh_ref, HIGH_PIECES, 16)):
        for _, z, x, first, count, step, at in pieces:
            known[z][row_slice(plane(x + shift) + first, count, step), :] = source[at : at + count, :]

    peaks = peaks_ref[0:8, :]
    for i in range(1, peaks_ref.shape[0] // 8):
        peaks = jnp.maximum(peaks, peaks_ref[8 * i : 8 * i + 8, :])
    upper = jnp.max(jnp.where(lane < 64, peaks, -jnp.inf))
    lower = jnp.max(jnp.where(lane < 64, -jnp.inf, peaks))
    step = jnp.full((1, 1), 2.0 * (REL_BOUND * (upper + lower)), F32)
    inverse = 1.0 / step

    def quantize(values, outer_low, inner_low, inner_high, outer_high):
        predicted = 0.5625 * (inner_low + inner_high) - 0.0625 * (outer_low + outer_high)
        code = code_of((values - predicted) * inverse)
        return code, predicted + step * code

    for x in range(-2, 19, 4):
        rows = [plane(x + d) + OWN_R - 4 for d in (0, -6, -2, 2, 6)]
        args = [known0[pl.ds(r, 8, stride=2), :] for r in rows]
        code, value = quantize(*args)
        known0[pl.ds(rows[0], 8, stride=2), :] = value
        codes0[pl.ds(rows[0], 8, stride=2), :] = code
    rows = [plane(-2 + d) + OWN_R + 12 for d in (0, -6, -2, 2, 6)]
    args = [known0[pl.ds(r, 6, stride=4 * ROWS), :] for r in rows]
    code, value = quantize(*args)
    known0[pl.ds(rows[0], 6, stride=4 * ROWS), :] = value

    for x in range(-2, 19, 2):
        first = plane(x) + OWN_R - 1
        args = [known0[pl.ds(first + d, 6, stride=2), :] for d in (0, -3, -1, 1, 3)]
        code, value = quantize(*args)
        known0[pl.ds(first, 6, stride=2), :] = value
        codes0[pl.ds(first, 6, stride=2), :] = code

    for x in range(-2, 19, 2):
        for first, count in ((OWN_R - 1, 8), (OWN_R + 7, 3)):
            rows = pl.ds(plane(x) + first, count)
            k = known0[rows, :]
            code, value = quantize(
                known2[rows, :], pltpu.roll(k, 1, 1), k, pltpu.roll(k, 127, 1), pltpu.roll(k, 126, 1)
            )
            known2[rows, :] = value
            codes2[rows, :] = code
    for x in range(0, 16, 4):
        codes0[pl.ds(plane(x) + OWN_R, 4, stride=2), :] = jnp.zeros((4, 128), F32)

    for x in range(1, 16, 2):
        for first, count in ((OWN_R - 1, 8), (OWN_R + 7, 3)):
            for z in range(2):
                args = [known[z][pl.ds(plane(x + d) + first, count), :] for d in (0, -3, -1, 1, 3)]
                code, value = quantize(*args)
                known[z][pl.ds(plane(x) + first, count), :] = value
                codes[z][pl.ds(plane(x) + first, count), :] = code

    for x in range(16):
        for z in range(2):
            base = plane(x) + OWN_R
            inner = known[z][pl.ds(base, 8), :]
            code, value = quantize(
                phase_ref[2 * z, pl.ds(16 * x + 1, 8, stride=2), :],
                known[z][pl.ds(base - 1, 8), :],
                inner,
                known[z][pl.ds(base + 1, 8), :],
                known[z][pl.ds(base + 2, 8), :],
            )
            full[z][pl.ds(16 * x, 8, stride=2), :] = inner
            full[z][pl.ds(16 * x + 1, 8, stride=2), :] = value
            fullc[z][pl.ds(16 * x, 8, stride=2), :] = codes[z][pl.ds(base, 8), :]
            fullc[z][pl.ds(16 * x + 1, 8, stride=2), :] = code
        for t in range(2):
            rows = slice(16 * x + 8 * t, 16 * x + 8 * t + 8)
            k0 = full0[rows, :]
            k2 = full2[rows, :]
            k0_next = pltpu.roll(k0, 127, 1)
            k2_next = pltpu.roll(k2, 127, 1)
            k2_last = pltpu.roll(k2, 1, 1)
            fullc1[rows, :], _ = quantize(phase_ref[1, rows, :], k2_last, k0, k2, k0_next)
            fullc3[rows, :], _ = quantize(phase_ref[3, rows, :], k0, k2, k0_next, k2_next)

    source = lax.broadcasted_iota(jnp.int32, (256, 256), 0)
    target = lax.broadcasted_iota(jnp.int32, (256, 256), 1)
    matrix = (target == 4 * (source % 64) + source // 64).astype(F32).astype(BF16)
    low_half = lax.broadcasted_iota(jnp.int32, (256, 128), 1) < 64
    parts = [fullc0[...], fullc1[...], fullc2[...], fullc3[...]]
    turned = [pltpu.roll(p, 64, 1) for p in parts]
    first = jnp.concatenate(
        [jnp.where(low_half, parts[0], turned[1]), jnp.where(low_half, parts[2], turned[3])], axis=1
    )
    second = jnp.concatenate(
        [jnp.where(low_half, turned[0], parts[1]), jnp.where(low_half, turned[2], parts[3])], axis=1
    )
    out_ref[:, :, 0:256] = permute_lanes(first, matrix).reshape(16, 16, 256)
    out_ref[:, :, 256:512] = permute_lanes(second, matrix).reshape(16, 16, 256)


def shards(snapshot):
    nx = lax.axis_size("gx")
    ny = lax.axis_size("gy")
    vmem = pl.BlockSpec(memory_space=pltpu.VMEM)
    block = snapshot.reshape(snapshot.shape[1:])
    params = pltpu.CompilerParams(vmem_limit_bytes=16 * 1024 * 1024)

    def shape(*dims):
        return jax.ShapeDtypeStruct(dims, F32)

    phases, low, high, peak = pl.pallas_call(
        prepare_kernel,
        in_specs=[vmem],
        out_specs=[vmem] * 4,
        out_shape=[shape(4, 256, 128), shape(LOW_COUNT, 128), shape(HIGH_COUNT, 128), shape(nx * ny, 128)],
        compiler_params=params,
        name="prepare",
    )(block)

    def shifted(array, axis, d):
        n = lax.axis_size(axis)
        return lax.ppermute(array, axis, [(i, (i + d) % n) for i in range(n)])

    peaks = lax.all_to_all(peak, AXES, 0, 0, tiled=True)
    ylow = shifted(low, "gy", 1)
    yhigh = shifted(high, "gy", -1)
    low_planes, high_planes = pl.pallas_call(
        join_kernel,
        in_specs=[vmem] * 3,
        out_specs=[vmem] * 2,
        out_shape=[shape(LOW_TOTAL, 128), shape(HIGH_TOTAL, 128)],
        scratch_shapes=[
            pltpu.VMEM((ROWS * len(LOW_PLANES), 128), F32),
            pltpu.VMEM((ROWS * len(HIGH_PLANES), 128), F32),
        ],
        compiler_params=params,
        name="join",
    )(phases, ylow, yhigh)
    xlow = shifted(low_planes, "gx", 1)
    xhigh = shifted(high_planes, "gx", -1)

    codes = pl.pallas_call(
        compress_kernel,
        in_specs=[vmem] * 6,
        out_specs=vmem,
        out_shape=shape(*block.shape),
        scratch_shapes=[pltpu.VMEM((PLANES * ROWS, 128), F32)] * 4 + [pltpu.VMEM((256, 128), F32)] * 6,
        compiler_params=params,
        name="compress",
    )(phases, ylow, yhigh, xlow, xhigh, peaks)
    return codes.reshape(snapshot.shape)


def solution(mesh):
    spec = P(None, "gx", "gy", None)
    return jax.shard_map(shards, mesh=mesh, in_specs=(spec,), out_specs=spec, check_vma=False)
```

```python
import jax
import jax.numpy as jnp
from jax import lax
from jax.experimental import pallas as pl
from jax.experimental.pallas import tpu as pltpu
from jax.sharding import PartitionSpec as P

REL_BOUND = 0.01
AXES = ("gx", "gy")

Q_COEFFS = (6.579714775085449, -12.986868858337402, 12.191614151000977, -6.570947170257568, 1.9706368446350098)

PLANES = 33
ROWS = 24
OWN_X = 8
OWN_R = 8

LOW_PLANES = ((0, 8), (0, 12), (0, 14), (1, 14))
HIGH_PLANES = ((0, 0), (0, 2), (1, 0), (1, 2), (0, 4), (0, 8))
LOW_ROWS = ((0, 14, 1), (1, 14, 1), (0, 8, 2), (0, 12, 2))
HIGH_ROWS = ((0, 0, 1), (1, 0, 1), (0, 2, 1), (1, 2, 1), (0, 4, 2), (0, 8, 2))
F32 = jnp.float32
BF16 = jnp.bfloat16
CHUNKS = 4
CHUNK_X = 16 // CHUNKS


TOTAL = 80


def packed_at(rows):
    at, places = 0, []
    for _, _, step in rows:
        places.append(at)
        at += 16 // step
    return places, at


LOW_AT, LOW_COUNT = packed_at(LOW_ROWS)
HIGH_AT, HIGH_COUNT = packed_at(HIGH_ROWS)
assert max(LOW_COUNT, HIGH_COUNT) <= TOTAL


def plane_pieces(planes, total):
    main, extra = [], []
    for i, (z, x) in enumerate(planes):
        if z == 1:
            main.append((i, z, x, 7, 8, 1))
            extra.append((i, z, x, 15, 3, 1))
            continue
        if x in (0, 2, 14):
            main.append((i, z, x, 4, 8, 1))
            main.append((i, z, x, 12, 8, 1))
        else:
            main.append((i, z, x, 4, 8, 2))
        extra.append((i, z, x, 20, 1, 1))
    at, pieces = 0, []
    for piece in main + extra:
        pieces.append(piece + (at,))
        at += piece[4]
    assert at <= total
    return pieces


LOW_PIECES = plane_pieces(LOW_PLANES, TOTAL)
HIGH_PIECES = plane_pieces(HIGH_PLANES, TOTAL)


def row_slice(first, count, step):
    return pl.ds(first, count) if step == 1 else pl.ds(first, count, stride=step)


def permute_lanes(values, matrix):
    first = values.astype(BF16)
    rest = values - first.astype(F32)
    second = rest.astype(BF16)
    third = (rest - second.astype(F32)).astype(BF16)
    parts = [jnp.dot(piece, matrix, preferred_element_type=F32) for piece in (first, second, third)]
    return parts[0] + (parts[1] + parts[2])


def phase_matrix(lanes, phases):
    source = lax.broadcasted_iota(jnp.int32, (lanes, 128), 0)
    target = lax.broadcasted_iota(jnp.int32, (lanes, 128), 1)
    parts = [(source == 4 * target + p).astype(F32).astype(BF16) for p in phases]
    return jnp.concatenate(parts, axis=1)


def swap_by_parity(axis, first_ref, second_ref):
    even = lax.rem(lax.axis_index(axis), 2) == 0
    first, second = first_ref[...], second_ref[...]
    return jnp.where(even, first, second), jnp.where(even, second, first)


def prepare_kernel(block_hbm, raw_ref, near_ref, far_ref, peak_hbm, peak_ref, split_ref, low_ref, high_ref, sems):
    copies = []
    for c in range(2):
        part = pl.ds(8 * c, 8)
        copies.append(pltpu.make_async_copy(block_hbm.at[part], raw_ref.at[part], sems.at[c]))
        copies[c].start()
    matrix = phase_matrix(512, (0, 2))

    highest = [None] * 4
    lowest = [None] * 4
    for c in range(2):
        copies[c].wait()
        for x in range(8 * c, 8 * c + 8):
            for t in range(2):
                for k in range(4):
                    chunk = raw_ref[x, 8 * t : 8 * t + 8, 128 * k : 128 * k + 128]
                    highest[k] = chunk if highest[k] is None else jnp.maximum(highest[k], chunk)
                    lowest[k] = chunk if lowest[k] is None else jnp.minimum(lowest[k], chunk)
    upper = jnp.maximum(jnp.maximum(highest[0], highest[1]), jnp.maximum(highest[2], highest[3]))
    lower = -jnp.minimum(jnp.minimum(lowest[0], lowest[1]), jnp.minimum(lowest[2], lowest[3]))
    lane = lax.broadcasted_iota(jnp.int32, (8, 128), 1)
    upper = jnp.maximum(upper, pltpu.roll(upper, 64, 1))
    lower = jnp.maximum(lower, pltpu.roll(lower, 64, 1))
    peak = jnp.where(lane < 64, upper, lower)
    for s in (4, 2, 1):
        peak = jnp.maximum(peak, pltpu.roll(peak, s, 0))
    for i in range(peak_ref.shape[0] // 8):
        peak_ref[8 * i : 8 * i + 8, :] = peak
    send = pltpu.make_async_copy(peak_ref, peak_hbm, sems.at[2])
    send.start()

    ys = sorted({y for _, y, _ in LOW_ROWS + HIGH_ROWS})
    stacked = [
        jnp.concatenate([raw_ref[8 * half : 8 * half + 8, y, 128 * k : 128 * k + 128] for k in range(4)], axis=1)
        for y in ys
        for half in range(2)
    ]
    split = permute_lanes(jnp.concatenate(stacked, axis=0), matrix)
    for z in range(2):
        split_ref[z] = split[:, 128 * z : 128 * z + 128]
    for ref, rows, ats in ((low_ref, LOW_ROWS, LOW_AT), (high_ref, HIGH_ROWS, HIGH_AT)):
        for (z, y, step), at in zip(rows, ats):
            ref[at : at + 16 // step, :] = split_ref[z, row_slice(16 * ys.index(y), 16 // step, step), :]
    low_ref[LOW_COUNT:TOTAL, :] = jnp.zeros((TOTAL - LOW_COUNT, 128), F32)
    near_ref[...], far_ref[...] = swap_by_parity("gy", low_ref, high_ref)
    send.wait()


def split_kernel(raw_ref, phase_ref):
    source = lax.broadcasted_iota(jnp.int32, (256, 256), 0)
    target = lax.broadcasted_iota(jnp.int32, (256, 256), 1)
    matrix = (source == 4 * (target % 64) + target // 64).astype(F32).astype(BF16)
    halves = [permute_lanes(raw_ref[:, :, 256 * h : 256 * h + 256].reshape(256, 256), matrix) for h in range(2)]
    low_half = lax.broadcasted_iota(jnp.int32, (256, 128), 1) < 64
    for j in range(2):
        a = halves[0][:, 128 * j : 128 * j + 128]
        b = halves[1][:, 128 * j : 128 * j + 128]
        phase_ref[2 * j] = jnp.where(low_half, a, pltpu.roll(b, 64, 1))
        phase_ref[2 * j + 1] = jnp.where(low_half, pltpu.roll(a, 64, 1), b)


def join_kernel(
    phase_ref, yfar_ref, ynear_ref, near_ref, far_ref, ylow_ref, yhigh_ref, low_ref, high_ref, low_planes, high_planes
):
    yhigh_ref[...], ylow_ref[...] = swap_by_parity("gy", ynear_ref, yfar_ref)
    for ref, planes, out, pieces in (
        (low_planes, LOW_PLANES, low_ref, LOW_PIECES),
        (high_planes, HIGH_PLANES, high_ref, HIGH_PIECES),
    ):
        for i, (z, x) in enumerate(planes):
            base = ROWS * i
            ref[base + OWN_R : base + OWN_R + 8, :] = phase_ref[2 * z, pl.ds(16 * x, 8, stride=2), :]
            for source, rows, places, shift in ((ylow_ref, LOW_ROWS, LOW_AT, -16), (yhigh_ref, HIGH_ROWS, HIGH_AT, 16)):
                for (zz, y, step), at in zip(rows, places):
                    if zz == z and x % step == 0:
                        r = base + OWN_R + (y + shift) // 2
                        ref[r : r + 1, :] = source[at + x // step : at + x // step + 1, :]
        for i, z, x, first, count, step, at in pieces:
            out[at : at + count, :] = ref[row_slice(ROWS * i + first, count, step), :]
    near_ref[...], far_ref[...] = swap_by_parity("gx", low_ref, high_ref)


def merge_phases(parts, lane):
    turned = [parts[0]] + [pltpu.roll(parts[p], 32 * p, 1) for p in (1, 2, 3)]
    quarter = lane // 32
    merged = []
    for k in range(4):
        block = turned[(3 - k) % 4]
        for q in range(3):
            block = jnp.where(quarter == q, turned[(q - k) % 4], block)
        order = 32 * ((lane % 4 + k) % 4) + lane // 4
        merged.append(jnp.take_along_axis(block, order, axis=1))
    return merged


def code_of(scaled):
    whole = jnp.round(scaled)
    r = scaled - whole
    s = r * r
    q = Q_COEFFS[-1]
    for c in Q_COEFFS[-2::-1]:
        q = q * s + c
    return whole + (r * s) * q


def compress_kernel(
    phase_ref, ylow_ref, yhigh_ref, xnear_ref, xfar_ref, peaks_ref, out_hbm,
    known0, known2, codes0, codes2, full0, full2, fullc0, fullc2, xlow_ref, xhigh_ref, out_ref, sems,
):
    lane = lax.broadcasted_iota(jnp.int32, (8, 128), 1)
    known = (known0, known2)
    codes = (codes0, codes2)
    full = (full0, full2)
    fullc = (fullc0, fullc2)

    def plane(x):
        return (x + OWN_X) * ROWS

    xhigh_ref[...], xlow_ref[...] = swap_by_parity("gx", xnear_ref, xfar_ref)
    for z in range(2):
        for x in range(16):
            base = plane(x) + OWN_R
            known[z][base : base + 8, :] = phase_ref[2 * z, pl.ds(16 * x, 8, stride=2), :]
    for source, rows, places, shift in ((ylow_ref, LOW_ROWS, LOW_AT, -16), (yhigh_ref, HIGH_ROWS, HIGH_AT, 16)):
        for (z, y, step), at in zip(rows, places):
            r = plane(0) + OWN_R + (y + shift) // 2
            for half in range(2 // step):
                known[z][pl.ds(r + 8 * half * ROWS, 8, stride=step * ROWS), :] = source[at + 8 * half : at + 8 * half + 8, :]
    for source, pieces, shift in ((xlow_ref, LOW_PIECES, -16), (xhigh_ref, HIGH_PIECES, 16)):
        for _, z, x, first, count, step, at in pieces:
            known[z][row_slice(plane(x + shift) + first, count, step), :] = source[at : at + count, :]

    peaks = peaks_ref[0:8, :]
    for i in range(1, peaks_ref.shape[0] // 8):
        peaks = jnp.maximum(peaks, peaks_ref[8 * i : 8 * i + 8, :])
    upper = jnp.max(jnp.where(lane < 64, peaks, -jnp.inf))
    lower = jnp.max(jnp.where(lane < 64, -jnp.inf, peaks))
    step = jnp.full((1, 1), 2.0 * (REL_BOUND * (upper + lower)), F32)
    inverse = 1.0 / step

    def quantize(values, outer_low, inner_low, inner_high, outer_high):
        predicted = 0.5625 * (inner_low + inner_high) - 0.0625 * (outer_low + outer_high)
        code = code_of((values - predicted) * inverse)
        return code, predicted + step * code

    for x in range(-2, 19, 4):
        rows = [plane(x + d) + OWN_R - 4 for d in (0, -6, -2, 2, 6)]
        args = [known0[pl.ds(r, 8, stride=2), :] for r in rows]
        code, value = quantize(*args)
        known0[pl.ds(rows[0], 8, stride=2), :] = value
        codes0[pl.ds(rows[0], 8, stride=2), :] = code
    rows = [plane(-2 + d) + OWN_R + 12 for d in (0, -6, -2, 2, 6)]
    args = [known0[pl.ds(r, 6, stride=4 * ROWS), :] for r in rows]
    code, value = quantize(*args)
    known0[pl.ds(rows[0], 6, stride=4 * ROWS), :] = value

    for x in range(-2, 19, 2):
        first = plane(x) + OWN_R - 1
        args = [known0[pl.ds(first + d, 6, stride=2), :] for d in (0, -3, -1, 1, 3)]
        code, value = quantize(*args)
        known0[pl.ds(first, 6, stride=2), :] = value
        codes0[pl.ds(first, 6, stride=2), :] = code

    for x in range(-2, 19, 2):
        for first, count in ((OWN_R - 1, 8), (OWN_R + 7, 3)):
            rows = pl.ds(plane(x) + first, count)
            k = known0[rows, :]
            code, value = quantize(
                known2[rows, :], pltpu.roll(k, 1, 1), k, pltpu.roll(k, 127, 1), pltpu.roll(k, 126, 1)
            )
            known2[rows, :] = value
            codes2[rows, :] = code
    for x in range(0, 16, 4):
        codes0[pl.ds(plane(x) + OWN_R, 4, stride=2), :] = jnp.zeros((4, 128), F32)

    for x in range(1, 16, 2):
        for first, count in ((OWN_R - 1, 8), (OWN_R + 7, 3)):
            for z in range(2):
                args = [known[z][pl.ds(plane(x + d) + first, count), :] for d in (0, -3, -1, 1, 3)]
                code, value = quantize(*args)
                known[z][pl.ds(plane(x) + first, count), :] = value
                codes[z][pl.ds(plane(x) + first, count), :] = code

    def last_steps(x):
        for z in range(2):
            base = plane(x) + OWN_R
            inner = known[z][pl.ds(base, 8), :]
            code, value = quantize(
                phase_ref[2 * z, pl.ds(16 * x + 1, 8, stride=2), :],
                known[z][pl.ds(base - 1, 8), :],
                inner,
                known[z][pl.ds(base + 1, 8), :],
                known[z][pl.ds(base + 2, 8), :],
            )
            full[z][pl.ds(16 * x, 8, stride=2), :] = inner
            full[z][pl.ds(16 * x + 1, 8, stride=2), :] = value
            fullc[z][pl.ds(16 * x, 8, stride=2), :] = codes[z][pl.ds(base, 8), :]
            fullc[z][pl.ds(16 * x + 1, 8, stride=2), :] = code
        for t in range(2):
            rows = slice(16 * x + 8 * t, 16 * x + 8 * t + 8)
            k0 = full0[rows, :]
            k2 = full2[rows, :]
            k0_next = pltpu.roll(k0, 127, 1)
            k2_next = pltpu.roll(k2, 127, 1)
            k2_last = pltpu.roll(k2, 1, 1)
            code1, _ = quantize(phase_ref[1, rows, :], k2_last, k0, k2, k0_next)
            code3, _ = quantize(phase_ref[3, rows, :], k0, k2, k0_next, k2_next)
            merged = merge_phases([fullc0[rows, :], code1, fullc2[rows, :], code3], lane)
            for k in range(4):
                out_ref[x, 8 * t : 8 * t + 8, 128 * k : 128 * k + 128] = merged[k]

    copies = []
    for c in range(CHUNKS):
        for x in range(c * CHUNK_X, c * CHUNK_X + CHUNK_X):
            last_steps(x)
        part = pl.ds(c * CHUNK_X, CHUNK_X)
        copies.append(pltpu.make_async_copy(out_ref.at[part], out_hbm.at[part], sems.at[c]))
        copies[c].start()
    for copy in copies:
        copy.wait()


def shards(snapshot):
    nx = lax.axis_size("gx")
    ny = lax.axis_size("gy")
    vmem = pl.BlockSpec(memory_space=pltpu.VMEM)
    hbm = pl.BlockSpec(memory_space=pltpu.HBM)
    block = snapshot.reshape(snapshot.shape[1:])
    params = pltpu.CompilerParams(vmem_limit_bytes=16 * 1024 * 1024)

    def shape(*dims):
        return jax.ShapeDtypeStruct(dims, F32)

    block = pltpu.with_memory_space_constraint(block, pltpu.HBM)
    raw, near, far, peak = pl.pallas_call(
        prepare_kernel,
        in_specs=[hbm],
        out_specs=[vmem] * 3 + [hbm],
        out_shape=[shape(*block.shape), shape(TOTAL, 128), shape(TOTAL, 128), shape(nx * ny, 128)],
        scratch_shapes=[
            pltpu.VMEM((nx * ny, 128), F32),
            pltpu.VMEM((2, 16 * 6, 128), F32),
            pltpu.VMEM((TOTAL, 128), F32),
            pltpu.VMEM((TOTAL, 128), F32),
            pltpu.SemaphoreType.DMA((3,)),
        ],
        compiler_params=params,
        name="prepare",
    )(block)
    phases = pl.pallas_call(
        split_kernel,
        in_specs=[vmem],
        out_specs=vmem,
        out_shape=shape(4, 256, 128),
        compiler_params=params,
        name="split",
    )(raw)

    def exchanged(array, axis, odd):
        n = lax.axis_size(axis)
        return lax.ppermute(array, axis, [(i, (i + (1 if i % 2 == odd else -1)) % n) for i in range(n)])

    peaks = lax.all_to_all(peak, AXES, 0, 0, tiled=True)
    yfar = exchanged(far, "gy", 1)
    ynear = exchanged(near, "gy", 0)
    near, far, ylow, yhigh = pl.pallas_call(
        join_kernel,
        in_specs=[vmem] * 3,
        out_specs=[vmem] * 4,
        out_shape=[shape(TOTAL, 128)] * 4,
        scratch_shapes=[
            pltpu.VMEM((TOTAL, 128), F32),
            pltpu.VMEM((TOTAL, 128), F32),
            pltpu.VMEM((ROWS * len(LOW_PLANES), 128), F32),
            pltpu.VMEM((ROWS * len(HIGH_PLANES), 128), F32),
        ],
        compiler_params=params,
        name="join",
    )(phases, yfar, ynear)
    xnear = exchanged(near, "gx", 0)
    xfar = exchanged(far, "gx", 1)

    codes = pl.pallas_call(
        compress_kernel,
        in_specs=[vmem] * 6,
        out_specs=hbm,
        out_shape=shape(*block.shape),
        scratch_shapes=[pltpu.VMEM((PLANES * ROWS, 128), F32)] * 4
        + [pltpu.VMEM((256, 128), F32)] * 4
        + [pltpu.VMEM((TOTAL, 128), F32)] * 2
        + [pltpu.VMEM(block.shape, F32), pltpu.SemaphoreType.DMA((CHUNKS,))],
        compiler_params=params,
        name="compress",
    )(phases, ylow, yhigh, xnear, xfar, peaks)
    return codes.reshape(snapshot.shape)


def solution(mesh):
    spec = P(None, "gx", "gy", None)
    return jax.shard_map(shards, mesh=mesh, in_specs=(spec,), out_specs=spec, check_vma=False)
```

```python
import jax
import jax.numpy as jnp
from jax import lax
from jax.experimental import pallas as pl
from jax.experimental.pallas import tpu as pltpu
from jax.sharding import PartitionSpec as P

REL_BOUND = 0.01
AXES = ("gx", "gy")

Q_COEFFS = (6.579714775085449, -12.986868858337402, 12.191614151000977, -6.570947170257568, 1.9706368446350098)

PLANES = 33
ROWS = 24
OWN_X = 8
OWN_R = 8

LOW_PLANES = ((0, 8), (0, 12), (0, 14), (1, 14))
HIGH_PLANES = ((0, 0), (0, 2), (1, 0), (1, 2), (0, 4), (0, 8))
LOW_ROWS = ((0, 14, 1), (1, 14, 1), (0, 8, 2), (0, 12, 2))
HIGH_ROWS = ((0, 0, 1), (1, 0, 1), (0, 2, 1), (1, 2, 1), (0, 4, 2), (0, 8, 2))
F32 = jnp.float32
BF16 = jnp.bfloat16
CHUNKS = 4
CHUNK_X = 16 // CHUNKS


TOTAL = 80


def packed_at(rows):
    at, places = 0, []
    for _, _, step in rows:
        places.append(at)
        at += 16 // step
    return places, at


LOW_AT, LOW_COUNT = packed_at(LOW_ROWS)
HIGH_AT, HIGH_COUNT = packed_at(HIGH_ROWS)
assert max(LOW_COUNT, HIGH_COUNT) <= TOTAL


def plane_pieces(planes, total):
    main, extra = [], []
    for i, (z, x) in enumerate(planes):
        if z == 1:
            main.append((i, z, x, 7, 8, 1))
            extra.append((i, z, x, 15, 3, 1))
            continue
        if x in (0, 2, 14):
            main.append((i, z, x, 4, 8, 1))
            main.append((i, z, x, 12, 8, 1))
        else:
            main.append((i, z, x, 4, 8, 2))
        extra.append((i, z, x, 20, 1, 1))
    at, pieces = 0, []
    for piece in main + extra:
        pieces.append(piece + (at,))
        at += piece[4]
    assert at <= total
    return pieces


LOW_PIECES = plane_pieces(LOW_PLANES, TOTAL)
HIGH_PIECES = plane_pieces(HIGH_PLANES, TOTAL)


def row_slice(first, count, step):
    return pl.ds(first, count) if step == 1 else pl.ds(first, count, stride=step)


def permute_lanes(values, matrix):
    first = values.astype(BF16)
    rest = values - first.astype(F32)
    second = rest.astype(BF16)
    third = (rest - second.astype(F32)).astype(BF16)
    parts = [jnp.dot(piece, matrix, preferred_element_type=F32) for piece in (first, second, third)]
    return parts[0] + (parts[1] + parts[2])


def phase_matrix(lanes, phases):
    source = lax.broadcasted_iota(jnp.int32, (lanes, 128), 0)
    target = lax.broadcasted_iota(jnp.int32, (lanes, 128), 1)
    parts = [(source == 4 * target + p).astype(F32).astype(BF16) for p in phases]
    return jnp.concatenate(parts, axis=1)


def swap_by_parity(axis, first_ref, second_ref):
    even = lax.rem(lax.axis_index(axis), 2) == 0
    first, second = first_ref[...], second_ref[...]
    return jnp.where(even, first, second), jnp.where(even, second, first)


def prepare_kernel(block_hbm, raw_ref, near_ref, far_ref, peak_hbm, peak_ref, split_ref, low_ref, high_ref, sems):
    copies = []
    for c in range(2):
        part = pl.ds(8 * c, 8)
        copies.append(pltpu.make_async_copy(block_hbm.at[part], raw_ref.at[part], sems.at[c]))
        copies[c].start()
    matrix = phase_matrix(512, (0, 2))

    highest = [None] * 4
    lowest = [None] * 4
    for c in range(2):
        copies[c].wait()
        for x in range(8 * c, 8 * c + 8):
            for t in range(2):
                for k in range(4):
                    chunk = raw_ref[x, 8 * t : 8 * t + 8, 128 * k : 128 * k + 128]
                    highest[k] = chunk if highest[k] is None else jnp.maximum(highest[k], chunk)
                    lowest[k] = chunk if lowest[k] is None else jnp.minimum(lowest[k], chunk)
    upper = jnp.maximum(jnp.maximum(highest[0], highest[1]), jnp.maximum(highest[2], highest[3]))
    lower = -jnp.minimum(jnp.minimum(lowest[0], lowest[1]), jnp.minimum(lowest[2], lowest[3]))
    lane = lax.broadcasted_iota(jnp.int32, (8, 128), 1)
    upper = jnp.maximum(upper, pltpu.roll(upper, 64, 1))
    lower = jnp.maximum(lower, pltpu.roll(lower, 64, 1))
    peak = jnp.where(lane < 64, upper, lower)
    for s in (4, 2, 1):
        peak = jnp.maximum(peak, pltpu.roll(peak, s, 0))
    for i in range(peak_ref.shape[0] // 8):
        peak_ref[8 * i : 8 * i + 8, :] = peak
    send = pltpu.make_async_copy(peak_ref, peak_hbm, sems.at[2])
    send.start()

    ys = sorted({y for _, y, _ in LOW_ROWS + HIGH_ROWS})
    stacked = [
        jnp.concatenate([raw_ref[8 * half : 8 * half + 8, y, 128 * k : 128 * k + 128] for k in range(4)], axis=1)
        for y in ys
        for half in range(2)
    ]
    split = permute_lanes(jnp.concatenate(stacked, axis=0), matrix)
    for z in range(2):
        split_ref[z] = split[:, 128 * z : 128 * z + 128]
    for ref, rows, ats in ((low_ref, LOW_ROWS, LOW_AT), (high_ref, HIGH_ROWS, HIGH_AT)):
        for (z, y, step), at in zip(rows, ats):
            ref[at : at + 16 // step, :] = split_ref[z, row_slice(16 * ys.index(y), 16 // step, step), :]
    low_ref[LOW_COUNT:TOTAL, :] = jnp.zeros((TOTAL - LOW_COUNT, 128), F32)
    near_ref[...], far_ref[...] = swap_by_parity("gy", low_ref, high_ref)
    send.wait()


def split_kernel(raw_ref, phase_ref):
    source = lax.broadcasted_iota(jnp.int32, (256, 256), 0)
    target = lax.broadcasted_iota(jnp.int32, (256, 256), 1)
    matrix = (source == 4 * (target % 64) + target // 64).astype(F32).astype(BF16)
    halves = [permute_lanes(raw_ref[:, :, 256 * h : 256 * h + 256].reshape(256, 256), matrix) for h in range(2)]
    low_half = lax.broadcasted_iota(jnp.int32, (256, 128), 1) < 64
    for j in range(2):
        a = halves[0][:, 128 * j : 128 * j + 128]
        b = halves[1][:, 128 * j : 128 * j + 128]
        phase_ref[2 * j] = jnp.where(low_half, a, pltpu.roll(b, 64, 1))
        phase_ref[2 * j + 1] = jnp.where(low_half, pltpu.roll(a, 64, 1), b)


def join_kernel(
    phase_ref, yfar_ref, ynear_ref, low_ref, high_ref, ylow_ref, yhigh_ref, low_planes, high_planes
):
    yhigh_ref[...], ylow_ref[...] = swap_by_parity("gy", ynear_ref, yfar_ref)
    for ref, planes, out, pieces in (
        (low_planes, LOW_PLANES, low_ref, LOW_PIECES),
        (high_planes, HIGH_PLANES, high_ref, HIGH_PIECES),
    ):
        for i, (z, x) in enumerate(planes):
            base = ROWS * i
            ref[base + OWN_R : base + OWN_R + 8, :] = phase_ref[2 * z, pl.ds(16 * x, 8, stride=2), :]
            for source, rows, places, shift in ((ylow_ref, LOW_ROWS, LOW_AT, -16), (yhigh_ref, HIGH_ROWS, HIGH_AT, 16)):
                for (zz, y, step), at in zip(rows, places):
                    if zz == z and x % step == 0:
                        r = base + OWN_R + (y + shift) // 2
                        ref[r : r + 1, :] = source[at + x // step : at + x // step + 1, :]
        for i, z, x, first, count, step, at in pieces:
            out[at : at + count, :] = ref[row_slice(ROWS * i + first, count, step), :]


def merge_phases(parts, lane):
    turned = [parts[0]] + [pltpu.roll(parts[p], 32 * p, 1) for p in (1, 2, 3)]
    quarter = lane // 32
    merged = []
    for k in range(4):
        block = turned[(3 - k) % 4]
        for q in range(3):
            block = jnp.where(quarter == q, turned[(q - k) % 4], block)
        order = 32 * ((lane % 4 + k) % 4) + lane // 4
        merged.append(jnp.take_along_axis(block, order, axis=1))
    return merged


def code_of(scaled):
    whole = jnp.round(scaled)
    r = scaled - whole
    s = r * r
    q = Q_COEFFS[-1]
    for c in Q_COEFFS[-2::-1]:
        q = q * s + c
    return whole + (r * s) * q


def compress_kernel(
    phase_ref, ylow_ref, yhigh_ref, xlow_ref, xhigh_ref, peaks_ref, out_hbm,
    known0, known2, codes0, codes2, full0, full2, fullc0, fullc2, out_ref, sems,
):
    lane = lax.broadcasted_iota(jnp.int32, (8, 128), 1)
    known = (known0, known2)
    codes = (codes0, codes2)
    full = (full0, full2)
    fullc = (fullc0, fullc2)

    def plane(x):
        return (x + OWN_X) * ROWS

    for z in range(2):
        for x in range(16):
            base = plane(x) + OWN_R
            known[z][base : base + 8, :] = phase_ref[2 * z, pl.ds(16 * x, 8, stride=2), :]
    for source, rows, places, shift in ((ylow_ref, LOW_ROWS, LOW_AT, -16), (yhigh_ref, HIGH_ROWS, HIGH_AT, 16)):
        for (z, y, step), at in zip(rows, places):
            r = plane(0) + OWN_R + (y + shift) // 2
            for half in range(2 // step):
                known[z][pl.ds(r + 8 * half * ROWS, 8, stride=step * ROWS), :] = source[at + 8 * half : at + 8 * half + 8, :]
    for source, pieces, shift in ((xlow_ref, LOW_PIECES, -16), (xhigh_ref, HIGH_PIECES, 16)):
        for _, z, x, first, count, step, at in pieces:
            known[z][row_slice(plane(x + shift) + first, count, step), :] = source[at : at + count, :]

    peaks = peaks_ref[0:8, :]
    for i in range(1, peaks_ref.shape[0] // 8):
        peaks = jnp.maximum(peaks, peaks_ref[8 * i : 8 * i + 8, :])
    upper = jnp.max(jnp.where(lane < 64, peaks, -jnp.inf))
    lower = jnp.max(jnp.where(lane < 64, -jnp.inf, peaks))
    step = jnp.full((1, 1), 2.0 * (REL_BOUND * (upper + lower)), F32)
    inverse = 1.0 / step

    def quantize(values, outer_low, inner_low, inner_high, outer_high):
        predicted = 0.5625 * (inner_low + inner_high) - 0.0625 * (outer_low + outer_high)
        code = code_of((values - predicted) * inverse)
        return code, predicted + step * code

    for x in range(-2, 19, 4):
        rows = [plane(x + d) + OWN_R - 4 for d in (0, -6, -2, 2, 6)]
        args = [known0[pl.ds(r, 8, stride=2), :] for r in rows]
        code, value = quantize(*args)
        known0[pl.ds(rows[0], 8, stride=2), :] = value
        codes0[pl.ds(rows[0], 8, stride=2), :] = code
    rows = [plane(-2 + d) + OWN_R + 12 for d in (0, -6, -2, 2, 6)]
    args = [known0[pl.ds(r, 6, stride=4 * ROWS), :] for r in rows]
    code, value = quantize(*args)
    known0[pl.ds(rows[0], 6, stride=4 * ROWS), :] = value

    for x in range(-2, 19, 2):
        first = plane(x) + OWN_R - 1
        args = [known0[pl.ds(first + d, 6, stride=2), :] for d in (0, -3, -1, 1, 3)]
        code, value = quantize(*args)
        known0[pl.ds(first, 6, stride=2), :] = value
        codes0[pl.ds(first, 6, stride=2), :] = code

    for x in range(-2, 19, 2):
        for first, count in ((OWN_R - 1, 8), (OWN_R + 7, 3)):
            rows = pl.ds(plane(x) + first, count)
            k = known0[rows, :]
            code, value = quantize(
                known2[rows, :], pltpu.roll(k, 1, 1), k, pltpu.roll(k, 127, 1), pltpu.roll(k, 126, 1)
            )
            known2[rows, :] = value
            codes2[rows, :] = code
    for x in range(0, 16, 4):
        codes0[pl.ds(plane(x) + OWN_R, 4, stride=2), :] = jnp.zeros((4, 128), F32)

    for x in range(1, 16, 2):
        for first, count in ((OWN_R - 1, 8), (OWN_R + 7, 3)):
            for z in range(2):
                args = [known[z][pl.ds(plane(x + d) + first, count), :] for d in (0, -3, -1, 1, 3)]
                code, value = quantize(*args)
                known[z][pl.ds(plane(x) + first, count), :] = value
                codes[z][pl.ds(plane(x) + first, count), :] = code

    def last_steps(x):
        for z in range(2):
            base = plane(x) + OWN_R
            inner = known[z][pl.ds(base, 8), :]
            code, value = quantize(
                phase_ref[2 * z, pl.ds(16 * x + 1, 8, stride=2), :],
                known[z][pl.ds(base - 1, 8), :],
                inner,
                known[z][pl.ds(base + 1, 8), :],
                known[z][pl.ds(base + 2, 8), :],
            )
            full[z][pl.ds(16 * x, 8, stride=2), :] = inner
            full[z][pl.ds(16 * x + 1, 8, stride=2), :] = value
            fullc[z][pl.ds(16 * x, 8, stride=2), :] = codes[z][pl.ds(base, 8), :]
            fullc[z][pl.ds(16 * x + 1, 8, stride=2), :] = code
        for t in range(2):
            rows = slice(16 * x + 8 * t, 16 * x + 8 * t + 8)
            k0 = full0[rows, :]
            k2 = full2[rows, :]
            k0_next = pltpu.roll(k0, 127, 1)
            k2_next = pltpu.roll(k2, 127, 1)
            k2_last = pltpu.roll(k2, 1, 1)
            code1, _ = quantize(phase_ref[1, rows, :], k2_last, k0, k2, k0_next)
            code3, _ = quantize(phase_ref[3, rows, :], k0, k2, k0_next, k2_next)
            merged = merge_phases([fullc0[rows, :], code1, fullc2[rows, :], code3], lane)
            for k in range(4):
                out_ref[x, 8 * t : 8 * t + 8, 128 * k : 128 * k + 128] = merged[k]

    copies = []
    for c in range(CHUNKS):
        for x in range(c * CHUNK_X, c * CHUNK_X + CHUNK_X):
            last_steps(x)
        part = pl.ds(c * CHUNK_X, CHUNK_X)
        copies.append(pltpu.make_async_copy(out_ref.at[part], out_hbm.at[part], sems.at[c]))
        copies[c].start()
    for copy in copies:
        copy.wait()


def shards(snapshot):
    nx = lax.axis_size("gx")
    ny = lax.axis_size("gy")
    vmem = pl.BlockSpec(memory_space=pltpu.VMEM)
    hbm = pl.BlockSpec(memory_space=pltpu.HBM)
    block = snapshot.reshape(snapshot.shape[1:])
    params = pltpu.CompilerParams(vmem_limit_bytes=16 * 1024 * 1024)

    def shape(*dims):
        return jax.ShapeDtypeStruct(dims, F32)

    block = pltpu.with_memory_space_constraint(block, pltpu.HBM)
    raw, near, far, peak = pl.pallas_call(
        prepare_kernel,
        in_specs=[hbm],
        out_specs=[vmem] * 3 + [hbm],
        out_shape=[shape(*block.shape), shape(TOTAL, 128), shape(TOTAL, 128), shape(nx * ny, 128)],
        scratch_shapes=[
            pltpu.VMEM((nx * ny, 128), F32),
            pltpu.VMEM((2, 16 * 6, 128), F32),
            pltpu.VMEM((TOTAL, 128), F32),
            pltpu.VMEM((TOTAL, 128), F32),
            pltpu.SemaphoreType.DMA((3,)),
        ],
        compiler_params=params,
        name="prepare",
    )(block)
    phases = pl.pallas_call(
        split_kernel,
        in_specs=[vmem],
        out_specs=vmem,
        out_shape=shape(4, 256, 128),
        compiler_params=params,
        name="split",
    )(raw)

    def shifted(array, axis, d):
        n = lax.axis_size(axis)
        return lax.ppermute(array, axis, [(i, (i + d) % n) for i in range(n)])

    def exchanged(array, axis, odd):
        n = lax.axis_size(axis)
        return lax.ppermute(array, axis, [(i, (i + (1 if i % 2 == odd else -1)) % n) for i in range(n)])

    peaks = lax.all_to_all(peak, AXES, 0, 0, tiled=True)
    yfar = exchanged(far, "gy", 1)
    ynear = exchanged(near, "gy", 0)
    low, high, ylow, yhigh = pl.pallas_call(
        join_kernel,
        in_specs=[vmem] * 3,
        out_specs=[vmem] * 4,
        out_shape=[shape(TOTAL, 128)] * 4,
        scratch_shapes=[
            pltpu.VMEM((ROWS * len(LOW_PLANES), 128), F32),
            pltpu.VMEM((ROWS * len(HIGH_PLANES), 128), F32),
        ],
        compiler_params=params,
        name="join",
    )(phases, yfar, ynear)
    xlow = shifted(low, "gx", 1)
    xhigh = shifted(high, "gx", -1)

    codes = pl.pallas_call(
        compress_kernel,
        in_specs=[vmem] * 6,
        out_specs=hbm,
        out_shape=shape(*block.shape),
        scratch_shapes=[pltpu.VMEM((PLANES * ROWS, 128), F32)] * 4
        + [pltpu.VMEM((256, 128), F32)] * 4
        + [pltpu.VMEM(block.shape, F32), pltpu.SemaphoreType.DMA((CHUNKS,))],
        compiler_params=params,
        name="compress",
    )(phases, ylow, yhigh, xlow, xhigh, peaks)
    return codes.reshape(snapshot.shape)


def solution(mesh):
    spec = P(None, "gx", "gy", None)
    return jax.shard_map(shards, mesh=mesh, in_specs=(spec,), out_specs=spec, check_vma=False)
```

```python
import jax
import jax.numpy as jnp
from jax import lax
from jax.experimental import pallas as pl
from jax.experimental.pallas import tpu as pltpu
from jax.sharding import PartitionSpec as P

REL_BOUND = 0.01
AXES = ("gx", "gy")

Q_COEFFS = (6.579714775085449, -12.986868858337402, 12.191614151000977, -6.570947170257568, 1.9706368446350098)

PLANES = 33
ROWS = 24
OWN_X = 8
OWN_R = 8

LOW_PLANES = ((0, 8), (0, 12), (0, 14), (1, 14))
HIGH_PLANES = ((0, 0), (0, 2), (1, 0), (1, 2), (0, 4), (0, 8))
LOW_ROWS = ((0, 14, 1), (1, 14, 1), (0, 8, 2), (0, 12, 2))
HIGH_ROWS = ((0, 0, 1), (1, 0, 1), (0, 2, 1), (1, 2, 1), (0, 4, 2), (0, 8, 2))
F32 = jnp.float32
BF16 = jnp.bfloat16
CHUNKS = 4
CHUNK_X = 16 // CHUNKS


TOTAL = 80


def packed_at(rows):
    at, places = 0, []
    for _, _, step in rows:
        places.append(at)
        at += 16 // step
    return places, at


LOW_AT, LOW_COUNT = packed_at(LOW_ROWS)
HIGH_AT, HIGH_COUNT = packed_at(HIGH_ROWS)
assert max(LOW_COUNT, HIGH_COUNT) <= TOTAL


def plane_pieces(planes, total):
    main, extra = [], []
    for i, (z, x) in enumerate(planes):
        if z == 1:
            main.append((i, z, x, 7, 8, 1))
            extra.append((i, z, x, 15, 3, 1))
            continue
        if x in (0, 2, 14):
            main.append((i, z, x, 4, 8, 1))
            main.append((i, z, x, 12, 8, 1))
        else:
            main.append((i, z, x, 4, 8, 2))
        extra.append((i, z, x, 20, 1, 1))
    at, pieces = 0, []
    for piece in main + extra:
        pieces.append(piece + (at,))
        at += piece[4]
    assert at <= total
    return pieces


LOW_PIECES = plane_pieces(LOW_PLANES, TOTAL)
HIGH_PIECES = plane_pieces(HIGH_PLANES, TOTAL)


def row_slice(first, count, step):
    return pl.ds(first, count) if step == 1 else pl.ds(first, count, stride=step)


def permute_lanes(values, matrix):
    first = values.astype(BF16)
    rest = values - first.astype(F32)
    second = rest.astype(BF16)
    third = (rest - second.astype(F32)).astype(BF16)
    parts = [jnp.dot(piece, matrix, preferred_element_type=F32) for piece in (first, second, third)]
    return parts[0] + (parts[1] + parts[2])


def phase_matrix(lanes, phases):
    source = lax.broadcasted_iota(jnp.int32, (lanes, 128), 0)
    target = lax.broadcasted_iota(jnp.int32, (lanes, 128), 1)
    parts = [(source == 4 * target + p).astype(F32).astype(BF16) for p in phases]
    return jnp.concatenate(parts, axis=1)


def swap_by_parity(axis, first_ref, second_ref):
    even = lax.rem(lax.axis_index(axis), 2) == 0
    first, second = first_ref[...], second_ref[...]
    return jnp.where(even, first, second), jnp.where(even, second, first)


def prepare_kernel(block_hbm, raw_ref, peak_hbm, peak_ref, sems):
    copies = []
    for c in range(2):
        part = pl.ds(8 * c, 8)
        copies.append(pltpu.make_async_copy(block_hbm.at[part], raw_ref.at[part], sems.at[c]))
        copies[c].start()

    highest = [None] * 4
    lowest = [None] * 4
    for c in range(2):
        copies[c].wait()
        for x in range(8 * c, 8 * c + 8):
            for t in range(2):
                for k in range(4):
                    chunk = raw_ref[x, 8 * t : 8 * t + 8, 128 * k : 128 * k + 128]
                    highest[k] = chunk if highest[k] is None else jnp.maximum(highest[k], chunk)
                    lowest[k] = chunk if lowest[k] is None else jnp.minimum(lowest[k], chunk)
    upper = jnp.maximum(jnp.maximum(highest[0], highest[1]), jnp.maximum(highest[2], highest[3]))
    lower = -jnp.minimum(jnp.minimum(lowest[0], lowest[1]), jnp.minimum(lowest[2], lowest[3]))
    lane = lax.broadcasted_iota(jnp.int32, (8, 128), 1)
    upper = jnp.maximum(upper, pltpu.roll(upper, 64, 1))
    lower = jnp.maximum(lower, pltpu.roll(lower, 64, 1))
    peak = jnp.where(lane < 64, upper, lower)
    for s in (4, 2, 1):
        peak = jnp.maximum(peak, pltpu.roll(peak, s, 0))
    for i in range(peak_ref.shape[0] // 8):
        peak_ref[8 * i : 8 * i + 8, :] = peak
    send = pltpu.make_async_copy(peak_ref, peak_hbm, sems.at[2])
    send.start()

    send.wait()


def rows_kernel(raw_ref, near_ref, far_ref, split_ref, low_ref, high_ref):
    matrix = phase_matrix(512, (0, 2))
    ys = sorted({y for _, y, _ in LOW_ROWS + HIGH_ROWS})
    stacked = [
        jnp.concatenate([raw_ref[8 * half : 8 * half + 8, y, 128 * k : 128 * k + 128] for k in range(4)], axis=1)
        for y in ys
        for half in range(2)
    ]
    split = permute_lanes(jnp.concatenate(stacked, axis=0), matrix)
    for z in range(2):
        split_ref[z] = split[:, 128 * z : 128 * z + 128]
    for ref, rows, ats in ((low_ref, LOW_ROWS, LOW_AT), (high_ref, HIGH_ROWS, HIGH_AT)):
        for (z, y, step), at in zip(rows, ats):
            ref[at : at + 16 // step, :] = split_ref[z, row_slice(16 * ys.index(y), 16 // step, step), :]
    low_ref[LOW_COUNT:TOTAL, :] = jnp.zeros((TOTAL - LOW_COUNT, 128), F32)
    near_ref[...], far_ref[...] = swap_by_parity("gy", low_ref, high_ref)


def split_kernel(raw_ref, phase_ref):
    source = lax.broadcasted_iota(jnp.int32, (256, 256), 0)
    target = lax.broadcasted_iota(jnp.int32, (256, 256), 1)
    matrix = (source == 4 * (target % 64) + target // 64).astype(F32).astype(BF16)
    halves = [permute_lanes(raw_ref[:, :, 256 * h : 256 * h + 256].reshape(256, 256), matrix) for h in range(2)]
    low_half = lax.broadcasted_iota(jnp.int32, (256, 128), 1) < 64
    for j in range(2):
        a = halves[0][:, 128 * j : 128 * j + 128]
        b = halves[1][:, 128 * j : 128 * j + 128]
        phase_ref[2 * j] = jnp.where(low_half, a, pltpu.roll(b, 64, 1))
        phase_ref[2 * j + 1] = jnp.where(low_half, pltpu.roll(a, 64, 1), b)


def join_kernel(
    phase_ref, yfar_ref, ynear_ref, low_ref, high_ref, ylow_ref, yhigh_ref, low_planes, high_planes
):
    yhigh_ref[...], ylow_ref[...] = swap_by_parity("gy", ynear_ref, yfar_ref)
    for ref, planes, out, pieces in (
        (low_planes, LOW_PLANES, low_ref, LOW_PIECES),
        (high_planes, HIGH_PLANES, high_ref, HIGH_PIECES),
    ):
        for i, (z, x) in enumerate(planes):
            base = ROWS * i
            ref[base + OWN_R : base + OWN_R + 8, :] = phase_ref[2 * z, pl.ds(16 * x, 8, stride=2), :]
            for source, rows, places, shift in ((ylow_ref, LOW_ROWS, LOW_AT, -16), (yhigh_ref, HIGH_ROWS, HIGH_AT, 16)):
                for (zz, y, step), at in zip(rows, places):
                    if zz == z and x % step == 0:
                        r = base + OWN_R + (y + shift) // 2
                        ref[r : r + 1, :] = source[at + x // step : at + x // step + 1, :]
        for i, z, x, first, count, step, at in pieces:
            out[at : at + count, :] = ref[row_slice(ROWS * i + first, count, step), :]


def merge_phases(parts, lane):
    turned = [parts[0]] + [pltpu.roll(parts[p], 32 * p, 1) for p in (1, 2, 3)]
    quarter = lane // 32
    merged = []
    for k in range(4):
        block = turned[(3 - k) % 4]
        for q in range(3):
            block = jnp.where(quarter == q, turned[(q - k) % 4], block)
        order = 32 * ((lane % 4 + k) % 4) + lane // 4
        merged.append(jnp.take_along_axis(block, order, axis=1))
    return merged


def code_of(scaled):
    whole = jnp.round(scaled)
    r = scaled - whole
    s = r * r
    q = Q_COEFFS[-1]
    for c in Q_COEFFS[-2::-1]:
        q = q * s + c
    return whole + (r * s) * q


def compress_kernel(
    phase_ref, ylow_ref, yhigh_ref, xlow_ref, xhigh_ref, peaks_ref, out_hbm,
    known0, known2, codes0, codes2, full0, full2, fullc0, fullc2, out_ref, sems,
):
    lane = lax.broadcasted_iota(jnp.int32, (8, 128), 1)
    known = (known0, known2)
    codes = (codes0, codes2)
    full = (full0, full2)
    fullc = (fullc0, fullc2)

    def plane(x):
        return (x + OWN_X) * ROWS

    for z in range(2):
        for x in range(16):
            base = plane(x) + OWN_R
            known[z][base : base + 8, :] = phase_ref[2 * z, pl.ds(16 * x, 8, stride=2), :]
    for source, rows, places, shift in ((ylow_ref, LOW_ROWS, LOW_AT, -16), (yhigh_ref, HIGH_ROWS, HIGH_AT, 16)):
        for (z, y, step), at in zip(rows, places):
            r = plane(0) + OWN_R + (y + shift) // 2
            for half in range(2 // step):
                known[z][pl.ds(r + 8 * half * ROWS, 8, stride=step * ROWS), :] = source[at + 8 * half : at + 8 * half + 8, :]
    for source, pieces, shift in ((xlow_ref, LOW_PIECES, -16), (xhigh_ref, HIGH_PIECES, 16)):
        for _, z, x, first, count, step, at in pieces:
            known[z][row_slice(plane(x + shift) + first, count, step), :] = source[at : at + count, :]

    peaks = peaks_ref[0:8, :]
    for i in range(1, peaks_ref.shape[0] // 8):
        peaks = jnp.maximum(peaks, peaks_ref[8 * i : 8 * i + 8, :])
    upper = jnp.max(jnp.where(lane < 64, peaks, -jnp.inf))
    lower = jnp.max(jnp.where(lane < 64, -jnp.inf, peaks))
    step = jnp.full((1, 1), 2.0 * (REL_BOUND * (upper + lower)), F32)
    inverse = 1.0 / step

    def quantize(values, outer_low, inner_low, inner_high, outer_high):
        predicted = 0.5625 * (inner_low + inner_high) - 0.0625 * (outer_low + outer_high)
        code = code_of((values - predicted) * inverse)
        return code, predicted + step * code

    for x in range(-2, 19, 4):
        rows = [plane(x + d) + OWN_R - 4 for d in (0, -6, -2, 2, 6)]
        args = [known0[pl.ds(r, 8, stride=2), :] for r in rows]
        code, value = quantize(*args)
        known0[pl.ds(rows[0], 8, stride=2), :] = value
        codes0[pl.ds(rows[0], 8, stride=2), :] = code
    rows = [plane(-2 + d) + OWN_R + 12 for d in (0, -6, -2, 2, 6)]
    args = [known0[pl.ds(r, 6, stride=4 * ROWS), :] for r in rows]
    code, value = quantize(*args)
    known0[pl.ds(rows[0], 6, stride=4 * ROWS), :] = value

    for x in range(-2, 19, 2):
        first = plane(x) + OWN_R - 1
        args = [known0[pl.ds(first + d, 6, stride=2), :] for d in (0, -3, -1, 1, 3)]
        code, value = quantize(*args)
        known0[pl.ds(first, 6, stride=2), :] = value
        codes0[pl.ds(first, 6, stride=2), :] = code

    for x in range(-2, 19, 2):
        for first, count in ((OWN_R - 1, 8), (OWN_R + 7, 3)):
            rows = pl.ds(plane(x) + first, count)
            k = known0[rows, :]
            code, value = quantize(
                known2[rows, :], pltpu.roll(k, 1, 1), k, pltpu.roll(k, 127, 1), pltpu.roll(k, 126, 1)
            )
            known2[rows, :] = value
            codes2[rows, :] = code
    for x in range(0, 16, 4):
        codes0[pl.ds(plane(x) + OWN_R, 4, stride=2), :] = jnp.zeros((4, 128), F32)

    for x in range(1, 16, 2):
        for first, count in ((OWN_R - 1, 8), (OWN_R + 7, 3)):
            for z in range(2):
                args = [known[z][pl.ds(plane(x + d) + first, count), :] for d in (0, -3, -1, 1, 3)]
                code, value = quantize(*args)
                known[z][pl.ds(plane(x) + first, count), :] = value
                codes[z][pl.ds(plane(x) + first, count), :] = code

    def last_steps(x):
        for z in range(2):
            base = plane(x) + OWN_R
            inner = known[z][pl.ds(base, 8), :]
            code, value = quantize(
                phase_ref[2 * z, pl.ds(16 * x + 1, 8, stride=2), :],
                known[z][pl.ds(base - 1, 8), :],
                inner,
                known[z][pl.ds(base + 1, 8), :],
                known[z][pl.ds(base + 2, 8), :],
            )
            full[z][pl.ds(16 * x, 8, stride=2), :] = inner
            full[z][pl.ds(16 * x + 1, 8, stride=2), :] = value
            fullc[z][pl.ds(16 * x, 8, stride=2), :] = codes[z][pl.ds(base, 8), :]
            fullc[z][pl.ds(16 * x + 1, 8, stride=2), :] = code
        for t in range(2):
            rows = slice(16 * x + 8 * t, 16 * x + 8 * t + 8)
            k0 = full0[rows, :]
            k2 = full2[rows, :]
            k0_next = pltpu.roll(k0, 127, 1)
            k2_next = pltpu.roll(k2, 127, 1)
            k2_last = pltpu.roll(k2, 1, 1)
            code1, _ = quantize(phase_ref[1, rows, :], k2_last, k0, k2, k0_next)
            code3, _ = quantize(phase_ref[3, rows, :], k0, k2, k0_next, k2_next)
            merged = merge_phases([fullc0[rows, :], code1, fullc2[rows, :], code3], lane)
            for k in range(4):
                out_ref[x, 8 * t : 8 * t + 8, 128 * k : 128 * k + 128] = merged[k]

    copies = []
    for c in range(CHUNKS):
        for x in range(c * CHUNK_X, c * CHUNK_X + CHUNK_X):
            last_steps(x)
        part = pl.ds(c * CHUNK_X, CHUNK_X)
        copies.append(pltpu.make_async_copy(out_ref.at[part], out_hbm.at[part], sems.at[c]))
        copies[c].start()
    for copy in copies:
        copy.wait()


def shards(snapshot):
    nx = lax.axis_size("gx")
    ny = lax.axis_size("gy")
    vmem = pl.BlockSpec(memory_space=pltpu.VMEM)
    hbm = pl.BlockSpec(memory_space=pltpu.HBM)
    block = snapshot.reshape(snapshot.shape[1:])
    params = pltpu.CompilerParams(vmem_limit_bytes=16 * 1024 * 1024)

    def shape(*dims):
        return jax.ShapeDtypeStruct(dims, F32)

    block = pltpu.with_memory_space_constraint(block, pltpu.HBM)
    raw, peak = pl.pallas_call(
        prepare_kernel,
        in_specs=[hbm],
        out_specs=[vmem, hbm],
        out_shape=[shape(*block.shape), shape(nx * ny, 128)],
        scratch_shapes=[pltpu.VMEM((nx * ny, 128), F32), pltpu.SemaphoreType.DMA((3,))],
        compiler_params=params,
        name="prepare",
    )(block)
    near, far = pl.pallas_call(
        rows_kernel,
        in_specs=[vmem],
        out_specs=[vmem] * 2,
        out_shape=[shape(TOTAL, 128)] * 2,
        scratch_shapes=[
            pltpu.VMEM((2, 16 * 6, 128), F32),
            pltpu.VMEM((TOTAL, 128), F32),
            pltpu.VMEM((TOTAL, 128), F32),
        ],
        compiler_params=params,
        name="rows",
    )(raw)
    phases = pl.pallas_call(
        split_kernel,
        in_specs=[vmem],
        out_specs=vmem,
        out_shape=shape(4, 256, 128),
        compiler_params=params,
        name="split",
    )(raw)

    def shifted(array, axis, d):
        n = lax.axis_size(axis)
        return lax.ppermute(array, axis, [(i, (i + d) % n) for i in range(n)])

    def exchanged(array, axis, odd):
        n = lax.axis_size(axis)
        return lax.ppermute(array, axis, [(i, (i + (1 if i % 2 == odd else -1)) % n) for i in range(n)])

    peaks = lax.all_to_all(peak, AXES, 0, 0, tiled=True)
    yfar = exchanged(far, "gy", 1)
    ynear = exchanged(near, "gy", 0)
    low, high, ylow, yhigh = pl.pallas_call(
        join_kernel,
        in_specs=[vmem] * 3,
        out_specs=[vmem] * 4,
        out_shape=[shape(TOTAL, 128)] * 4,
        scratch_shapes=[
            pltpu.VMEM((ROWS * len(LOW_PLANES), 128), F32),
            pltpu.VMEM((ROWS * len(HIGH_PLANES), 128), F32),
        ],
        compiler_params=params,
        name="join",
    )(phases, yfar, ynear)
    xlow = shifted(low, "gx", 1)
    xhigh = shifted(high, "gx", -1)

    codes = pl.pallas_call(
        compress_kernel,
        in_specs=[vmem] * 6,
        out_specs=hbm,
        out_shape=shape(*block.shape),
        scratch_shapes=[pltpu.VMEM((PLANES * ROWS, 128), F32)] * 4
        + [pltpu.VMEM((256, 128), F32)] * 4
        + [pltpu.VMEM(block.shape, F32), pltpu.SemaphoreType.DMA((CHUNKS,))],
        compiler_params=params,
        name="compress",
    )(phases, ylow, yhigh, xlow, xhigh, peaks)
    return codes.reshape(snapshot.shape)


def solution(mesh):
    spec = P(None, "gx", "gy", None)
    return jax.shard_map(shards, mesh=mesh, in_specs=(spec,), out_specs=spec, check_vma=False)
```

```python
import jax
import jax.numpy as jnp
from jax import lax
from jax.experimental import pallas as pl
from jax.experimental.pallas import tpu as pltpu
from jax.sharding import PartitionSpec as P

REL_BOUND = 0.01
AXES = ("gx", "gy")

Q_COEFFS = (6.579714775085449, -12.986868858337402, 12.191614151000977, -6.570947170257568, 1.9706368446350098)

PLANES = 33
ROWS = 24
OWN_X = 8
OWN_R = 8

LOW_PLANES = ((0, 8), (0, 12), (0, 14), (1, 14))
HIGH_PLANES = ((0, 0), (0, 2), (1, 0), (1, 2), (0, 4), (0, 8))
LOW_ROWS = ((0, 14, 1), (1, 14, 1), (0, 8, 2), (0, 12, 2))
HIGH_ROWS = ((0, 0, 1), (1, 0, 1), (0, 2, 1), (1, 2, 1), (0, 4, 2), (0, 8, 2))
F32 = jnp.float32
BF16 = jnp.bfloat16
CHUNKS = 4
CHUNK_X = 16 // CHUNKS


TOTAL = 80


def packed_at(rows):
    at, places = 0, []
    for _, _, step in rows:
        places.append(at)
        at += 16 // step
    return places, at


LOW_AT, LOW_COUNT = packed_at(LOW_ROWS)
HIGH_AT, HIGH_COUNT = packed_at(HIGH_ROWS)
assert max(LOW_COUNT, HIGH_COUNT) <= TOTAL


def plane_pieces(planes, total):
    main, extra = [], []
    for i, (z, x) in enumerate(planes):
        if z == 1:
            main.append((i, z, x, 7, 8, 1))
            extra.append((i, z, x, 15, 3, 1))
            continue
        if x in (0, 2, 14):
            main.append((i, z, x, 4, 8, 1))
            main.append((i, z, x, 12, 8, 1))
        else:
            main.append((i, z, x, 4, 8, 2))
        extra.append((i, z, x, 20, 1, 1))
    at, pieces = 0, []
    for piece in main + extra:
        pieces.append(piece + (at,))
        at += piece[4]
    assert at <= total
    return pieces


LOW_PIECES = plane_pieces(LOW_PLANES, 48)
HIGH_PIECES = plane_pieces(HIGH_PLANES, TOTAL)


def row_slice(first, count, step):
    return pl.ds(first, count) if step == 1 else pl.ds(first, count, stride=step)


def permute_lanes(values, matrix):
    first = values.astype(BF16)
    rest = values - first.astype(F32)
    second = rest.astype(BF16)
    third = (rest - second.astype(F32)).astype(BF16)
    parts = [jnp.dot(piece, matrix, preferred_element_type=F32) for piece in (first, second, third)]
    return parts[0] + (parts[1] + parts[2])


def phase_matrix(lanes, phases):
    source = lax.broadcasted_iota(jnp.int32, (lanes, 128), 0)
    target = lax.broadcasted_iota(jnp.int32, (lanes, 128), 1)
    parts = [(source == 4 * target + p).astype(F32).astype(BF16) for p in phases]
    return jnp.concatenate(parts, axis=1)


def swap_by_parity(axis, first_ref, second_ref):
    even = lax.rem(lax.axis_index(axis), 2) == 0
    first, second = first_ref[...], second_ref[...]
    return jnp.where(even, first, second), jnp.where(even, second, first)


def prepare_kernel(block_hbm, raw_ref, peak_hbm, peak_ref, sems):
    copies = []
    for c in range(2):
        part = pl.ds(8 * c, 8)
        copies.append(pltpu.make_async_copy(block_hbm.at[part], raw_ref.at[part], sems.at[c]))
        copies[c].start()

    highest = [None] * 4
    lowest = [None] * 4
    for c in range(2):
        copies[c].wait()
        for x in range(8 * c, 8 * c + 8):
            for t in range(2):
                for k in range(4):
                    chunk = raw_ref[x, 8 * t : 8 * t + 8, 128 * k : 128 * k + 128]
                    highest[k] = chunk if highest[k] is None else jnp.maximum(highest[k], chunk)
                    lowest[k] = chunk if lowest[k] is None else jnp.minimum(lowest[k], chunk)
    upper = jnp.maximum(jnp.maximum(highest[0], highest[1]), jnp.maximum(highest[2], highest[3]))
    lower = -jnp.minimum(jnp.minimum(lowest[0], lowest[1]), jnp.minimum(lowest[2], lowest[3]))
    lane = lax.broadcasted_iota(jnp.int32, (8, 128), 1)
    upper = jnp.maximum(upper, pltpu.roll(upper, 64, 1))
    lower = jnp.maximum(lower, pltpu.roll(lower, 64, 1))
    peak = jnp.where(lane < 64, upper, lower)
    for s in (4, 2, 1):
        peak = jnp.maximum(peak, pltpu.roll(peak, s, 0))
    for i in range(peak_ref.shape[0] // 8):
        peak_ref[8 * i : 8 * i + 8, :] = peak
    send = pltpu.make_async_copy(peak_ref, peak_hbm, sems.at[2])
    send.start()

    send.wait()


def rows_kernel(raw_ref, near_ref, far_ref, split_ref, low_ref, high_ref):
    matrix = phase_matrix(512, (0, 2))
    ys = sorted({y for _, y, _ in LOW_ROWS + HIGH_ROWS})
    stacked = [
        jnp.concatenate([raw_ref[8 * half : 8 * half + 8, y, 128 * k : 128 * k + 128] for k in range(4)], axis=1)
        for y in ys
        for half in range(2)
    ]
    split = permute_lanes(jnp.concatenate(stacked, axis=0), matrix)
    for z in range(2):
        split_ref[z] = split[:, 128 * z : 128 * z + 128]
    for ref, rows, ats in ((low_ref, LOW_ROWS, LOW_AT), (high_ref, HIGH_ROWS, HIGH_AT)):
        for (z, y, step), at in zip(rows, ats):
            ref[at : at + 16 // step, :] = split_ref[z, row_slice(16 * ys.index(y), 16 // step, step), :]
    low_ref[LOW_COUNT:TOTAL, :] = jnp.zeros((TOTAL - LOW_COUNT, 128), F32)
    near_ref[...], far_ref[...] = swap_by_parity("gy", low_ref, high_ref)


def split_kernel(raw_ref, phase_ref):
    source = lax.broadcasted_iota(jnp.int32, (256, 256), 0)
    target = lax.broadcasted_iota(jnp.int32, (256, 256), 1)
    matrix = (source == 4 * (target % 64) + target // 64).astype(F32).astype(BF16)
    halves = [permute_lanes(raw_ref[:, :, 256 * h : 256 * h + 256].reshape(256, 256), matrix) for h in range(2)]
    low_half = lax.broadcasted_iota(jnp.int32, (256, 128), 1) < 64
    for j in range(2):
        a = halves[0][:, 128 * j : 128 * j + 128]
        b = halves[1][:, 128 * j : 128 * j + 128]
        phase_ref[2 * j] = jnp.where(low_half, a, pltpu.roll(b, 64, 1))
        phase_ref[2 * j + 1] = jnp.where(low_half, pltpu.roll(a, 64, 1), b)


def join_kernel(
    phase_ref, yfar_ref, ynear_ref, low_ref, high_ref, ylow_ref, yhigh_ref, low_planes, high_planes
):
    yhigh_ref[...], ylow_ref[...] = swap_by_parity("gy", ynear_ref, yfar_ref)
    for ref, planes, out, pieces in (
        (low_planes, LOW_PLANES, low_ref, LOW_PIECES),
        (high_planes, HIGH_PLANES, high_ref, HIGH_PIECES),
    ):
        for i, (z, x) in enumerate(planes):
            base = ROWS * i
            ref[base + OWN_R : base + OWN_R + 8, :] = phase_ref[2 * z, pl.ds(16 * x, 8, stride=2), :]
            for source, rows, places, shift in ((ylow_ref, LOW_ROWS, LOW_AT, -16), (yhigh_ref, HIGH_ROWS, HIGH_AT, 16)):
                for (zz, y, step), at in zip(rows, places):
                    if zz == z and x % step == 0:
                        r = base + OWN_R + (y + shift) // 2
                        ref[r : r + 1, :] = source[at + x // step : at + x // step + 1, :]
        for i, z, x, first, count, step, at in pieces:
            out[at : at + count, :] = ref[row_slice(ROWS * i + first, count, step), :]


def relay_kernel(source_ref, target_ref):
    target_ref[...] = source_ref[...]


def merge_phases(parts, lane):
    turned = [parts[0]] + [pltpu.roll(parts[p], 32 * p, 1) for p in (1, 2, 3)]
    quarter = lane // 32
    merged = []
    for k in range(4):
        block = turned[(3 - k) % 4]
        for q in range(3):
            block = jnp.where(quarter == q, turned[(q - k) % 4], block)
        order = 32 * ((lane % 4 + k) % 4) + lane // 4
        merged.append(jnp.take_along_axis(block, order, axis=1))
    return merged


def code_of(scaled):
    whole = jnp.round(scaled)
    r = scaled - whole
    s = r * r
    q = Q_COEFFS[-1]
    for c in Q_COEFFS[-2::-1]:
        q = q * s + c
    return whole + (r * s) * q


def compress_kernel(
    phase_ref, ylow_ref, yhigh_ref, xlow_ref, xhigh_ref, peaks_ref, out_hbm,
    known0, known2, codes0, codes2, full0, full2, fullc0, fullc2, out_ref, sems,
):
    lane = lax.broadcasted_iota(jnp.int32, (8, 128), 1)
    known = (known0, known2)
    codes = (codes0, codes2)
    full = (full0, full2)
    fullc = (fullc0, fullc2)

    def plane(x):
        return (x + OWN_X) * ROWS

    for z in range(2):
        for x in range(16):
            base = plane(x) + OWN_R
            known[z][base : base + 8, :] = phase_ref[2 * z, pl.ds(16 * x, 8, stride=2), :]
    for source, rows, places, shift in ((ylow_ref, LOW_ROWS, LOW_AT, -16), (yhigh_ref, HIGH_ROWS, HIGH_AT, 16)):
        for (z, y, step), at in zip(rows, places):
            r = plane(0) + OWN_R + (y + shift) // 2
            for half in range(2 // step):
                known[z][pl.ds(r + 8 * half * ROWS, 8, stride=step * ROWS), :] = source[at + 8 * half : at + 8 * half + 8, :]
    for source, pieces, shift in ((xlow_ref, LOW_PIECES, -16), (xhigh_ref, HIGH_PIECES, 16)):
        for _, z, x, first, count, step, at in pieces:
            known[z][row_slice(plane(x + shift) + first, count, step), :] = source[at : at + count, :]

    peaks = peaks_ref[0:8, :]
    for i in range(1, peaks_ref.shape[0] // 8):
        peaks = jnp.maximum(peaks, peaks_ref[8 * i : 8 * i + 8, :])
    upper = jnp.max(jnp.where(lane < 64, peaks, -jnp.inf))
    lower = jnp.max(jnp.where(lane < 64, -jnp.inf, peaks))
    step = jnp.full((1, 1), 2.0 * (REL_BOUND * (upper + lower)), F32)
    inverse = 1.0 / step

    def quantize(values, outer_low, inner_low, inner_high, outer_high):
        predicted = 0.5625 * (inner_low + inner_high) - 0.0625 * (outer_low + outer_high)
        code = code_of((values - predicted) * inverse)
        return code, predicted + step * code

    for x in range(-2, 19, 4):
        rows = [plane(x + d) + OWN_R - 4 for d in (0, -6, -2, 2, 6)]
        args = [known0[pl.ds(r, 8, stride=2), :] for r in rows]
        code, value = quantize(*args)
        known0[pl.ds(rows[0], 8, stride=2), :] = value
        codes0[pl.ds(rows[0], 8, stride=2), :] = code
    rows = [plane(-2 + d) + OWN_R + 12 for d in (0, -6, -2, 2, 6)]
    args = [known0[pl.ds(r, 6, stride=4 * ROWS), :] for r in rows]
    code, value = quantize(*args)
    known0[pl.ds(rows[0], 6, stride=4 * ROWS), :] = value

    for x in range(-2, 19, 2):
        first = plane(x) + OWN_R - 1
        args = [known0[pl.ds(first + d, 6, stride=2), :] for d in (0, -3, -1, 1, 3)]
        code, value = quantize(*args)
        known0[pl.ds(first, 6, stride=2), :] = value
        codes0[pl.ds(first, 6, stride=2), :] = code

    for x in range(-2, 19, 2):
        for first, count in ((OWN_R - 1, 8), (OWN_R + 7, 3)):
            rows = pl.ds(plane(x) + first, count)
            k = known0[rows, :]
            code, value = quantize(
                known2[rows, :], pltpu.roll(k, 1, 1), k, pltpu.roll(k, 127, 1), pltpu.roll(k, 126, 1)
            )
            known2[rows, :] = value
            codes2[rows, :] = code
    for x in range(0, 16, 4):
        codes0[pl.ds(plane(x) + OWN_R, 4, stride=2), :] = jnp.zeros((4, 128), F32)

    for x in range(1, 16, 2):
        for first, count in ((OWN_R - 1, 8), (OWN_R + 7, 3)):
            for z in range(2):
                args = [known[z][pl.ds(plane(x + d) + first, count), :] for d in (0, -3, -1, 1, 3)]
                code, value = quantize(*args)
                known[z][pl.ds(plane(x) + first, count), :] = value
                codes[z][pl.ds(plane(x) + first, count), :] = code

    def last_steps(x):
        for z in range(2):
            base = plane(x) + OWN_R
            inner = known[z][pl.ds(base, 8), :]
            code, value = quantize(
                phase_ref[2 * z, pl.ds(16 * x + 1, 8, stride=2), :],
                known[z][pl.ds(base - 1, 8), :],
                inner,
                known[z][pl.ds(base + 1, 8), :],
                known[z][pl.ds(base + 2, 8), :],
            )
            full[z][pl.ds(16 * x, 8, stride=2), :] = inner
            full[z][pl.ds(16 * x + 1, 8, stride=2), :] = value
            fullc[z][pl.ds(16 * x, 8, stride=2), :] = codes[z][pl.ds(base, 8), :]
            fullc[z][pl.ds(16 * x + 1, 8, stride=2), :] = code
        for t in range(2):
            rows = slice(16 * x + 8 * t, 16 * x + 8 * t + 8)
            k0 = full0[rows, :]
            k2 = full2[rows, :]
            k0_next = pltpu.roll(k0, 127, 1)
            k2_next = pltpu.roll(k2, 127, 1)
            k2_last = pltpu.roll(k2, 1, 1)
            code1, _ = quantize(phase_ref[1, rows, :], k2_last, k0, k2, k0_next)
            code3, _ = quantize(phase_ref[3, rows, :], k0, k2, k0_next, k2_next)
            merged = merge_phases([fullc0[rows, :], code1, fullc2[rows, :], code3], lane)
            for k in range(4):
                out_ref[x, 8 * t : 8 * t + 8, 128 * k : 128 * k + 128] = merged[k]

    copies = []
    for c in range(CHUNKS):
        for x in range(c * CHUNK_X, c * CHUNK_X + CHUNK_X):
            last_steps(x)
        part = pl.ds(c * CHUNK_X, CHUNK_X)
        copies.append(pltpu.make_async_copy(out_ref.at[part], out_hbm.at[part], sems.at[c]))
        copies[c].start()
    for copy in copies:
        copy.wait()


def shards(snapshot):
    nx = lax.axis_size("gx")
    ny = lax.axis_size("gy")
    vmem = pl.BlockSpec(memory_space=pltpu.VMEM)
    hbm = pl.BlockSpec(memory_space=pltpu.HBM)
    block = snapshot.reshape(snapshot.shape[1:])
    params = pltpu.CompilerParams(vmem_limit_bytes=16 * 1024 * 1024)

    def shape(*dims):
        return jax.ShapeDtypeStruct(dims, F32)

    block = pltpu.with_memory_space_constraint(block, pltpu.HBM)
    raw, peak = pl.pallas_call(
        prepare_kernel,
        in_specs=[hbm],
        out_specs=[vmem, hbm],
        out_shape=[shape(*block.shape), shape(nx * ny, 128)],
        scratch_shapes=[pltpu.VMEM((nx * ny, 128), F32), pltpu.SemaphoreType.DMA((3,))],
        compiler_params=params,
        name="prepare",
    )(block)
    near, far = pl.pallas_call(
        rows_kernel,
        in_specs=[vmem],
        out_specs=[vmem] * 2,
        out_shape=[shape(TOTAL, 128)] * 2,
        scratch_shapes=[
            pltpu.VMEM((2, 16 * 6, 128), F32),
            pltpu.VMEM((TOTAL, 128), F32),
            pltpu.VMEM((TOTAL, 128), F32),
        ],
        compiler_params=params,
        name="rows",
    )(raw)
    phases = pl.pallas_call(
        split_kernel,
        in_specs=[vmem],
        out_specs=vmem,
        out_shape=shape(4, 256, 128),
        compiler_params=params,
        name="split",
    )(raw)

    def shifted(array, axis, d):
        n = lax.axis_size(axis)
        return lax.ppermute(array, axis, [(i, (i + d) % n) for i in range(n)])

    def exchanged(array, axis, odd):
        n = lax.axis_size(axis)
        return lax.ppermute(array, axis, [(i, (i + (1 if i % 2 == odd else -1)) % n) for i in range(n)])

    peaks = lax.all_to_all(peak, AXES, 0, 0, tiled=True)
    yfar = exchanged(far, "gy", 1)
    ynear = exchanged(near, "gy", 0)
    low, high, ylow, yhigh = pl.pallas_call(
        join_kernel,
        in_specs=[vmem] * 3,
        out_specs=[vmem] * 4,
        out_shape=[shape(48, 128)] + [shape(TOTAL, 128)] * 3,
        scratch_shapes=[
            pltpu.VMEM((ROWS * len(LOW_PLANES), 128), F32),
            pltpu.VMEM((ROWS * len(HIGH_PLANES), 128), F32),
        ],
        compiler_params=params,
        name="join",
    )(phases, yfar, ynear)
    xlow = shifted(low, "gx", 1)
    xhigh = shifted(high, "gx", -1)

    xlow = pl.pallas_call(
        relay_kernel,
        in_specs=[vmem],
        out_specs=vmem,
        out_shape=shape(48, 128),
        compiler_params=params,
        cost_estimate=pl.CostEstimate(flops=2 * 10**9, bytes_accessed=10**6, transcendentals=0),
        name="relay",
    )(xlow)
    codes = pl.pallas_call(
        compress_kernel,
        in_specs=[vmem] * 6,
        out_specs=hbm,
        out_shape=shape(*block.shape),
        scratch_shapes=[pltpu.VMEM((PLANES * ROWS, 128), F32)] * 4
        + [pltpu.VMEM((256, 128), F32)] * 4
        + [pltpu.VMEM(block.shape, F32), pltpu.SemaphoreType.DMA((CHUNKS,))],
        compiler_params=params,
        name="compress",
    )(phases, ylow, yhigh, xlow, xhigh, peaks)
    return codes.reshape(snapshot.shape)


def solution(mesh):
    spec = P(None, "gx", "gy", None)
    return jax.shard_map(shards, mesh=mesh, in_specs=(spec,), out_specs=spec, check_vma=False)
```

```python
import jax
import jax.numpy as jnp
from jax import lax
from jax.experimental import pallas as pl
from jax.experimental.pallas import tpu as pltpu
from jax.sharding import PartitionSpec as P

REL_BOUND = 0.01
AXES = ("gx", "gy")

Q_COEFFS = (6.579714775085449, -12.986868858337402, 12.191614151000977, -6.570947170257568, 1.9706368446350098)

PLANES = 33
ROWS = 24
OWN_X = 8
OWN_R = 8

LOW_PLANES = ((0, 8), (0, 12), (0, 14), (1, 14))
HIGH_PLANES = ((0, 0), (0, 2), (1, 0), (1, 2), (0, 4), (0, 8))
LOW_ROWS = ((0, 14, 1), (1, 14, 1), (0, 8, 2), (0, 12, 2))
HIGH_ROWS = ((0, 0, 1), (1, 0, 1), (0, 2, 1), (1, 2, 1), (0, 4, 2), (0, 8, 2))
F32 = jnp.float32
BF16 = jnp.bfloat16
CHUNKS = 4
CHUNK_X = 16 // CHUNKS


TOTAL = 80


def packed_at(rows):
    at, places = 0, []
    for _, _, step in rows:
        places.append(at)
        at += 16 // step
    return places, at


LOW_AT, LOW_COUNT = packed_at(LOW_ROWS)
HIGH_AT, HIGH_COUNT = packed_at(HIGH_ROWS)
assert max(LOW_COUNT, HIGH_COUNT) <= TOTAL


def plane_pieces(planes, total):
    main, extra = [], []
    for i, (z, x) in enumerate(planes):
        if z == 1:
            main.append((i, z, x, 7, 8, 1))
            extra.append((i, z, x, 15, 3, 1))
            continue
        if x in (0, 2, 14):
            main.append((i, z, x, 4, 8, 1))
            main.append((i, z, x, 12, 8, 1))
        else:
            main.append((i, z, x, 4, 8, 2))
        extra.append((i, z, x, 20, 1, 1))
    at, pieces = 0, []
    for piece in main + extra:
        pieces.append(piece + (at,))
        at += piece[4]
    assert at <= total
    return pieces


LOW_PIECES = plane_pieces(LOW_PLANES, 48)
HIGH_PIECES = plane_pieces(HIGH_PLANES, TOTAL)


def row_slice(first, count, step):
    return pl.ds(first, count) if step == 1 else pl.ds(first, count, stride=step)


def permute_lanes(values, matrix):
    first = values.astype(BF16)
    rest = values - first.astype(F32)
    second = rest.astype(BF16)
    third = (rest - second.astype(F32)).astype(BF16)
    parts = [jnp.dot(piece, matrix, preferred_element_type=F32) for piece in (first, second, third)]
    return parts[0] + (parts[1] + parts[2])


def phase_matrix(lanes, phases):
    source = lax.broadcasted_iota(jnp.int32, (lanes, 128), 0)
    target = lax.broadcasted_iota(jnp.int32, (lanes, 128), 1)
    parts = [(source == 4 * target + p).astype(F32).astype(BF16) for p in phases]
    return jnp.concatenate(parts, axis=1)


def swap_by_parity(axis, first_ref, second_ref):
    even = lax.rem(lax.axis_index(axis), 2) == 0
    first, second = first_ref[...], second_ref[...]
    return jnp.where(even, first, second), jnp.where(even, second, first)


def prepare_kernel(block_hbm, raw_ref, peak_hbm, peak_ref, sems):
    copies = []
    for c in range(2):
        part = pl.ds(8 * c, 8)
        copies.append(pltpu.make_async_copy(block_hbm.at[part], raw_ref.at[part], sems.at[c]))
        copies[c].start()

    highest = [None] * 4
    lowest = [None] * 4
    for c in range(2):
        copies[c].wait()
        for x in range(8 * c, 8 * c + 8):
            for t in range(2):
                for k in range(4):
                    chunk = raw_ref[x, 8 * t : 8 * t + 8, 128 * k : 128 * k + 128]
                    highest[k] = chunk if highest[k] is None else jnp.maximum(highest[k], chunk)
                    lowest[k] = chunk if lowest[k] is None else jnp.minimum(lowest[k], chunk)
    upper = jnp.maximum(jnp.maximum(highest[0], highest[1]), jnp.maximum(highest[2], highest[3]))
    lower = -jnp.minimum(jnp.minimum(lowest[0], lowest[1]), jnp.minimum(lowest[2], lowest[3]))
    lane = lax.broadcasted_iota(jnp.int32, (8, 128), 1)
    upper = jnp.maximum(upper, pltpu.roll(upper, 64, 1))
    lower = jnp.maximum(lower, pltpu.roll(lower, 64, 1))
    peak = jnp.where(lane < 64, upper, lower)
    for s in (4, 2, 1):
        peak = jnp.maximum(peak, pltpu.roll(peak, s, 0))
    for i in range(peak_ref.shape[0] // 8):
        peak_ref[8 * i : 8 * i + 8, :] = peak
    send = pltpu.make_async_copy(peak_ref, peak_hbm, sems.at[2])
    send.start()

    send.wait()


def rows_kernel(raw_ref, near_ref, far_ref, split_ref, low_ref, high_ref):
    matrix = phase_matrix(512, (0, 2))
    ys = sorted({y for _, y, _ in LOW_ROWS + HIGH_ROWS})
    stacked = [
        jnp.concatenate([raw_ref[8 * half : 8 * half + 8, y, 128 * k : 128 * k + 128] for k in range(4)], axis=1)
        for y in ys
        for half in range(2)
    ]
    split = permute_lanes(jnp.concatenate(stacked, axis=0), matrix)
    for z in range(2):
        split_ref[z] = split[:, 128 * z : 128 * z + 128]
    for ref, rows, ats in ((low_ref, LOW_ROWS, LOW_AT), (high_ref, HIGH_ROWS, HIGH_AT)):
        for (z, y, step), at in zip(rows, ats):
            ref[at : at + 16 // step, :] = split_ref[z, row_slice(16 * ys.index(y), 16 // step, step), :]
    low_ref[LOW_COUNT:TOTAL, :] = jnp.zeros((TOTAL - LOW_COUNT, 128), F32)
    near_ref[...], far_ref[...] = swap_by_parity("gy", low_ref, high_ref)


def split_kernel(raw_ref, phase_ref):
    source = lax.broadcasted_iota(jnp.int32, (256, 256), 0)
    target = lax.broadcasted_iota(jnp.int32, (256, 256), 1)
    matrix = (source == 4 * (target % 64) + target // 64).astype(F32).astype(BF16)
    halves = [permute_lanes(raw_ref[:, :, 256 * h : 256 * h + 256].reshape(256, 256), matrix) for h in range(2)]
    low_half = lax.broadcasted_iota(jnp.int32, (256, 128), 1) < 64
    for j in range(2):
        a = halves[0][:, 128 * j : 128 * j + 128]
        b = halves[1][:, 128 * j : 128 * j + 128]
        phase_ref[2 * j] = jnp.where(low_half, a, pltpu.roll(b, 64, 1))
        phase_ref[2 * j + 1] = jnp.where(low_half, pltpu.roll(a, 64, 1), b)


def join_kernel(
    phase_ref, yfar_ref, ynear_ref, low_ref, high_ref, ylow_ref, yhigh_ref, low_planes, high_planes
):
    yhigh_ref[...], ylow_ref[...] = swap_by_parity("gy", ynear_ref, yfar_ref)
    for ref, planes, out, pieces in (
        (low_planes, LOW_PLANES, low_ref, LOW_PIECES),
        (high_planes, HIGH_PLANES, high_ref, HIGH_PIECES),
    ):
        for i, (z, x) in enumerate(planes):
            base = ROWS * i
            ref[base + OWN_R : base + OWN_R + 8, :] = phase_ref[2 * z, pl.ds(16 * x, 8, stride=2), :]
            for source, rows, places, shift in ((ylow_ref, LOW_ROWS, LOW_AT, -16), (yhigh_ref, HIGH_ROWS, HIGH_AT, 16)):
                for (zz, y, step), at in zip(rows, places):
                    if zz == z and x % step == 0:
                        r = base + OWN_R + (y + shift) // 2
                        ref[r : r + 1, :] = source[at + x // step : at + x // step + 1, :]
        for i, z, x, first, count, step, at in pieces:
            out[at : at + count, :] = ref[row_slice(ROWS * i + first, count, step), :]


def relay_kernel(source_ref, target_ref):
    target_ref[...] = source_ref[...]


def merge_phases(parts, lane):
    turned = [parts[0]] + [pltpu.roll(parts[p], 32 * p, 1) for p in (1, 2, 3)]
    quarter = lane // 32
    merged = []
    for k in range(4):
        block = turned[(3 - k) % 4]
        for q in range(3):
            block = jnp.where(quarter == q, turned[(q - k) % 4], block)
        order = 32 * ((lane % 4 + k) % 4) + lane // 4
        merged.append(jnp.take_along_axis(block, order, axis=1))
    return merged


def code_of(scaled):
    whole = jnp.round(scaled)
    r = scaled - whole
    s = r * r
    c0, c1, c2, c3, c4 = Q_COEFFS
    ss = s * s
    q = (c0 + c1 * s) + ss * ((c2 + c3 * s) + c4 * ss)
    return whole + (r * s) * q


def compress_kernel(
    phase_ref, ylow_ref, yhigh_ref, xlow_ref, xhigh_ref, peaks_ref, out_hbm,
    known0, known2, codes0, codes2, full0, full2, fullc0, fullc2, out_ref, sems,
):
    lane = lax.broadcasted_iota(jnp.int32, (8, 128), 1)
    known = (known0, known2)
    codes = (codes0, codes2)
    full = (full0, full2)
    fullc = (fullc0, fullc2)

    def plane(x):
        return (x + OWN_X) * ROWS

    for z in range(2):
        for x in range(16):
            base = plane(x) + OWN_R
            known[z][base : base + 8, :] = phase_ref[2 * z, pl.ds(16 * x, 8, stride=2), :]
    for source, rows, places, shift in ((ylow_ref, LOW_ROWS, LOW_AT, -16), (yhigh_ref, HIGH_ROWS, HIGH_AT, 16)):
        for (z, y, step), at in zip(rows, places):
            r = plane(0) + OWN_R + (y + shift) // 2
            for half in range(2 // step):
                known[z][pl.ds(r + 8 * half * ROWS, 8, stride=step * ROWS), :] = source[at + 8 * half : at + 8 * half + 8, :]
    for source, pieces, shift in ((xlow_ref, LOW_PIECES, -16), (xhigh_ref, HIGH_PIECES, 16)):
        for _, z, x, first, count, step, at in pieces:
            known[z][row_slice(plane(x + shift) + first, count, step), :] = source[at : at + count, :]

    peaks = peaks_ref[0:8, :]
    for i in range(1, peaks_ref.shape[0] // 8):
        peaks = jnp.maximum(peaks, peaks_ref[8 * i : 8 * i + 8, :])
    upper = jnp.max(jnp.where(lane < 64, peaks, -jnp.inf))
    lower = jnp.max(jnp.where(lane < 64, -jnp.inf, peaks))
    step = jnp.full((1, 1), 2.0 * (REL_BOUND * (upper + lower)), F32)
    inverse = 1.0 / step

    def quantize(values, outer_low, inner_low, inner_high, outer_high):
        predicted = 0.5625 * (inner_low + inner_high) - 0.0625 * (outer_low + outer_high)
        code = code_of((values - predicted) * inverse)
        return code, predicted + step * code

    for x in range(-2, 19, 4):
        rows = [plane(x + d) + OWN_R - 4 for d in (0, -6, -2, 2, 6)]
        args = [known0[pl.ds(r, 8, stride=2), :] for r in rows]
        code, value = quantize(*args)
        known0[pl.ds(rows[0], 8, stride=2), :] = value
        codes0[pl.ds(rows[0], 8, stride=2), :] = code
    rows = [plane(-2 + d) + OWN_R + 12 for d in (0, -6, -2, 2, 6)]
    args = [known0[pl.ds(r, 6, stride=4 * ROWS), :] for r in rows]
    code, value = quantize(*args)
    known0[pl.ds(rows[0], 6, stride=4 * ROWS), :] = value

    for x in range(-2, 19, 2):
        first = plane(x) + OWN_R - 1
        args = [known0[pl.ds(first + d, 6, stride=2), :] for d in (0, -3, -1, 1, 3)]
        code, value = quantize(*args)
        known0[pl.ds(first, 6, stride=2), :] = value
        codes0[pl.ds(first, 6, stride=2), :] = code

    for x in range(-2, 19, 2):
        for first, count in ((OWN_R - 1, 8), (OWN_R + 7, 3)):
            rows = pl.ds(plane(x) + first, count)
            k = known0[rows, :]
            code, value = quantize(
                known2[rows, :], pltpu.roll(k, 1, 1), k, pltpu.roll(k, 127, 1), pltpu.roll(k, 126, 1)
            )
            known2[rows, :] = value
            codes2[rows, :] = code
    for x in range(0, 16, 4):
        codes0[pl.ds(plane(x) + OWN_R, 4, stride=2), :] = jnp.zeros((4, 128), F32)

    for x in range(1, 16, 2):
        for first, count in ((OWN_R - 1, 8), (OWN_R + 7, 3)):
            for z in range(2):
                args = [known[z][pl.ds(plane(x + d) + first, count), :] for d in (0, -3, -1, 1, 3)]
                code, value = quantize(*args)
                known[z][pl.ds(plane(x) + first, count), :] = value
                codes[z][pl.ds(plane(x) + first, count), :] = code

    def last_steps(x):
        for z in range(2):
            base = plane(x) + OWN_R
            inner = known[z][pl.ds(base, 8), :]
            code, value = quantize(
                phase_ref[2 * z, pl.ds(16 * x + 1, 8, stride=2), :],
                known[z][pl.ds(base - 1, 8), :],
                inner,
                known[z][pl.ds(base + 1, 8), :],
                known[z][pl.ds(base + 2, 8), :],
            )
            full[z][pl.ds(16 * x, 8, stride=2), :] = inner
            full[z][pl.ds(16 * x + 1, 8, stride=2), :] = value
            fullc[z][pl.ds(16 * x, 8, stride=2), :] = codes[z][pl.ds(base, 8), :]
            fullc[z][pl.ds(16 * x + 1, 8, stride=2), :] = code
        for t in range(2):
            rows = slice(16 * x + 8 * t, 16 * x + 8 * t + 8)
            k0 = full0[rows, :]
            k2 = full2[rows, :]
            k0_next = pltpu.roll(k0, 127, 1)
            k2_next = pltpu.roll(k2, 127, 1)
            k2_last = pltpu.roll(k2, 1, 1)
            code1, _ = quantize(phase_ref[1, rows, :], k2_last, k0, k2, k0_next)
            code3, _ = quantize(phase_ref[3, rows, :], k0, k2, k0_next, k2_next)
            merged = merge_phases([fullc0[rows, :], code1, fullc2[rows, :], code3], lane)
            for k in range(4):
                out_ref[x, 8 * t : 8 * t + 8, 128 * k : 128 * k + 128] = merged[k]

    copies = []
    for c in range(CHUNKS):
        for x in range(c * CHUNK_X, c * CHUNK_X + CHUNK_X):
            last_steps(x)
        part = pl.ds(c * CHUNK_X, CHUNK_X)
        copies.append(pltpu.make_async_copy(out_ref.at[part], out_hbm.at[part], sems.at[c]))
        copies[c].start()
    for copy in copies:
        copy.wait()


def shards(snapshot):
    nx = lax.axis_size("gx")
    ny = lax.axis_size("gy")
    vmem = pl.BlockSpec(memory_space=pltpu.VMEM)
    hbm = pl.BlockSpec(memory_space=pltpu.HBM)
    block = snapshot.reshape(snapshot.shape[1:])
    params = pltpu.CompilerParams(vmem_limit_bytes=16 * 1024 * 1024)

    def shape(*dims):
        return jax.ShapeDtypeStruct(dims, F32)

    block = pltpu.with_memory_space_constraint(block, pltpu.HBM)
    raw, peak = pl.pallas_call(
        prepare_kernel,
        in_specs=[hbm],
        out_specs=[vmem, hbm],
        out_shape=[shape(*block.shape), shape(nx * ny, 128)],
        scratch_shapes=[pltpu.VMEM((nx * ny, 128), F32), pltpu.SemaphoreType.DMA((3,))],
        compiler_params=params,
        name="prepare",
    )(block)
    near, far = pl.pallas_call(
        rows_kernel,
        in_specs=[vmem],
        out_specs=[vmem] * 2,
        out_shape=[shape(TOTAL, 128)] * 2,
        scratch_shapes=[
            pltpu.VMEM((2, 16 * 6, 128), F32),
            pltpu.VMEM((TOTAL, 128), F32),
            pltpu.VMEM((TOTAL, 128), F32),
        ],
        compiler_params=params,
        name="rows",
    )(raw)
    phases = pl.pallas_call(
        split_kernel,
        in_specs=[vmem],
        out_specs=vmem,
        out_shape=shape(4, 256, 128),
        compiler_params=params,
        name="split",
    )(raw)

    def shifted(array, axis, d):
        n = lax.axis_size(axis)
        return lax.ppermute(array, axis, [(i, (i + d) % n) for i in range(n)])

    def exchanged(array, axis, odd):
        n = lax.axis_size(axis)
        return lax.ppermute(array, axis, [(i, (i + (1 if i % 2 == odd else -1)) % n) for i in range(n)])

    peaks = lax.all_to_all(peak, AXES, 0, 0, tiled=True)
    yfar = exchanged(far, "gy", 1)
    ynear = exchanged(near, "gy", 0)
    low, high, ylow, yhigh = pl.pallas_call(
        join_kernel,
        in_specs=[vmem] * 3,
        out_specs=[vmem] * 4,
        out_shape=[shape(48, 128)] + [shape(TOTAL, 128)] * 3,
        scratch_shapes=[
            pltpu.VMEM((ROWS * len(LOW_PLANES), 128), F32),
            pltpu.VMEM((ROWS * len(HIGH_PLANES), 128), F32),
        ],
        compiler_params=params,
        name="join",
    )(phases, yfar, ynear)
    xlow = shifted(low, "gx", 1)
    xhigh = shifted(high, "gx", -1)

    xlow = pl.pallas_call(
        relay_kernel,
        in_specs=[vmem],
        out_specs=vmem,
        out_shape=shape(48, 128),
        compiler_params=params,
        cost_estimate=pl.CostEstimate(flops=2 * 10**9, bytes_accessed=10**6, transcendentals=0),
        name="relay",
    )(xlow)
    codes = pl.pallas_call(
        compress_kernel,
        in_specs=[vmem] * 6,
        out_specs=hbm,
        out_shape=shape(*block.shape),
        scratch_shapes=[pltpu.VMEM((PLANES * ROWS, 128), F32)] * 4
        + [pltpu.VMEM((256, 128), F32)] * 4
        + [pltpu.VMEM(block.shape, F32), pltpu.SemaphoreType.DMA((CHUNKS,))],
        compiler_params=params,
        name="compress",
    )(phases, ylow, yhigh, xlow, xhigh, peaks)
    return codes.reshape(snapshot.shape)


def solution(mesh):
    spec = P(None, "gx", "gy", None)
    return jax.shard_map(shards, mesh=mesh, in_specs=(spec,), out_specs=spec, check_vma=False)
```

```python
import jax
import jax.numpy as jnp
from jax import lax
from jax.experimental import pallas as pl
from jax.experimental.pallas import tpu as pltpu
from jax.sharding import PartitionSpec as P

REL_BOUND = 0.01
AXES = ("gx", "gy")

Q_COEFFS = (6.579714775085449, -12.986868858337402, 12.191614151000977, -6.570947170257568, 1.9706368446350098)

PLANES = 33
ROWS = 24
OWN_X = 8
OWN_R = 8

LOW_PLANES = ((0, 8), (0, 12), (0, 14), (1, 14))
HIGH_PLANES = ((0, 0), (0, 2), (1, 0), (1, 2), (0, 4), (0, 8))
LOW_ROWS = ((0, 14, 1), (1, 14, 1), (0, 8, 2), (0, 12, 2))
HIGH_ROWS = ((0, 0, 1), (1, 0, 1), (0, 2, 1), (1, 2, 1), (0, 4, 2), (0, 8, 2))
F32 = jnp.float32
BF16 = jnp.bfloat16
CHUNKS = 4
CHUNK_X = 16 // CHUNKS


TOTAL = 80


def packed_at(rows):
    at, places = 0, []
    for _, _, step in rows:
        places.append(at)
        at += 16 // step
    return places, at


LOW_AT, LOW_COUNT = packed_at(LOW_ROWS)
HIGH_AT, HIGH_COUNT = packed_at(HIGH_ROWS)
assert max(LOW_COUNT, HIGH_COUNT) <= TOTAL


def plane_pieces(planes, total):
    main, extra = [], []
    for i, (z, x) in enumerate(planes):
        if z == 1:
            main.append((i, z, x, 7, 8, 1))
            extra.append((i, z, x, 15, 3, 1))
            continue
        if x in (0, 2, 14):
            main.append((i, z, x, 4, 8, 1))
            main.append((i, z, x, 12, 8, 1))
        else:
            main.append((i, z, x, 4, 8, 2))
        extra.append((i, z, x, 20, 1, 1))
    at, pieces = 0, []
    for piece in main + extra:
        pieces.append(piece + (at,))
        at += piece[4]
    assert at <= total
    return pieces


LOW_PIECES = plane_pieces(LOW_PLANES, 48)
HIGH_PIECES = plane_pieces(HIGH_PLANES, TOTAL)


def row_slice(first, count, step):
    return pl.ds(first, count) if step == 1 else pl.ds(first, count, stride=step)


def permute_lanes(values, matrix):
    first = values.astype(BF16)
    rest = values - first.astype(F32)
    second = rest.astype(BF16)
    third = (rest - second.astype(F32)).astype(BF16)
    parts = [jnp.dot(piece, matrix, preferred_element_type=F32) for piece in (first, second, third)]
    return parts[0] + (parts[1] + parts[2])


def phase_matrix(lanes, phases):
    source = lax.broadcasted_iota(jnp.int32, (lanes, 128), 0)
    target = lax.broadcasted_iota(jnp.int32, (lanes, 128), 1)
    parts = [(source == 4 * target + p).astype(F32).astype(BF16) for p in phases]
    return jnp.concatenate(parts, axis=1)


def swap_by_parity(axis, first_ref, second_ref):
    even = lax.rem(lax.axis_index(axis), 2) == 0
    first, second = first_ref[...], second_ref[...]
    return jnp.where(even, first, second), jnp.where(even, second, first)


def prepare_kernel(block_hbm, raw_ref, peak_hbm, peak_ref, sems):
    copies = []
    for c in range(2):
        part = pl.ds(8 * c, 8)
        copies.append(pltpu.make_async_copy(block_hbm.at[part], raw_ref.at[part], sems.at[c]))
        copies[c].start()

    highest = [None] * 4
    lowest = [None] * 4
    for c in range(2):
        copies[c].wait()
        for x in range(8 * c, 8 * c + 8):
            for t in range(2):
                for k in range(4):
                    chunk = raw_ref[x, 8 * t : 8 * t + 8, 128 * k : 128 * k + 128]
                    highest[k] = chunk if highest[k] is None else jnp.maximum(highest[k], chunk)
                    lowest[k] = chunk if lowest[k] is None else jnp.minimum(lowest[k], chunk)
    upper = jnp.maximum(jnp.maximum(highest[0], highest[1]), jnp.maximum(highest[2], highest[3]))
    lower = -jnp.minimum(jnp.minimum(lowest[0], lowest[1]), jnp.minimum(lowest[2], lowest[3]))
    lane = lax.broadcasted_iota(jnp.int32, (8, 128), 1)
    upper = jnp.maximum(upper, pltpu.roll(upper, 64, 1))
    lower = jnp.maximum(lower, pltpu.roll(lower, 64, 1))
    peak = jnp.where(lane < 64, upper, lower)
    for s in (4, 2, 1):
        peak = jnp.maximum(peak, pltpu.roll(peak, s, 0))
    for i in range(peak_ref.shape[0] // 8):
        peak_ref[8 * i : 8 * i + 8, :] = peak
    send = pltpu.make_async_copy(peak_ref, peak_hbm, sems.at[2])
    send.start()

    send.wait()


def rows_kernel(raw_ref, near_ref, far_ref, split_ref, low_ref, high_ref):
    matrix = phase_matrix(512, (0, 2))
    ys = sorted({y for _, y, _ in LOW_ROWS + HIGH_ROWS})
    stacked = [
        jnp.concatenate([raw_ref[8 * half : 8 * half + 8, y, 128 * k : 128 * k + 128] for k in range(4)], axis=1)
        for y in ys
        for half in range(2)
    ]
    split = permute_lanes(jnp.concatenate(stacked, axis=0), matrix)
    for z in range(2):
        split_ref[z] = split[:, 128 * z : 128 * z + 128]
    for ref, rows, ats in ((low_ref, LOW_ROWS, LOW_AT), (high_ref, HIGH_ROWS, HIGH_AT)):
        for (z, y, step), at in zip(rows, ats):
            ref[at : at + 16 // step, :] = split_ref[z, row_slice(16 * ys.index(y), 16 // step, step), :]
    low_ref[LOW_COUNT:TOTAL, :] = jnp.zeros((TOTAL - LOW_COUNT, 128), F32)
    near_ref[...], far_ref[...] = swap_by_parity("gy", low_ref, high_ref)


def split_kernel(raw_ref, phase_ref):
    source = lax.broadcasted_iota(jnp.int32, (256, 256), 0)
    target = lax.broadcasted_iota(jnp.int32, (256, 256), 1)
    matrix = (source == 4 * (target % 64) + target // 64).astype(F32).astype(BF16)
    halves = [permute_lanes(raw_ref[:, :, 256 * h : 256 * h + 256].reshape(256, 256), matrix) for h in range(2)]
    low_half = lax.broadcasted_iota(jnp.int32, (256, 128), 1) < 64
    for j in range(2):
        a = halves[0][:, 128 * j : 128 * j + 128]
        b = halves[1][:, 128 * j : 128 * j + 128]
        phase_ref[2 * j] = jnp.where(low_half, a, pltpu.roll(b, 64, 1))
        phase_ref[2 * j + 1] = jnp.where(low_half, pltpu.roll(a, 64, 1), b)


def join_kernel(
    phase_ref, yfar_ref, ynear_ref, low_ref, high_ref, ylow_ref, yhigh_ref, low_planes, high_planes
):
    yhigh_ref[...], ylow_ref[...] = swap_by_parity("gy", ynear_ref, yfar_ref)
    for ref, planes, out, pieces in (
        (low_planes, LOW_PLANES, low_ref, LOW_PIECES),
        (high_planes, HIGH_PLANES, high_ref, HIGH_PIECES),
    ):
        for i, (z, x) in enumerate(planes):
            base = ROWS * i
            ref[base + OWN_R : base + OWN_R + 8, :] = phase_ref[2 * z, pl.ds(16 * x, 8, stride=2), :]
            for source, rows, places, shift in ((ylow_ref, LOW_ROWS, LOW_AT, -16), (yhigh_ref, HIGH_ROWS, HIGH_AT, 16)):
                for (zz, y, step), at in zip(rows, places):
                    if zz == z and x % step == 0:
                        r = base + OWN_R + (y + shift) // 2
                        ref[r : r + 1, :] = source[at + x // step : at + x // step + 1, :]
        for i, z, x, first, count, step, at in pieces:
            out[at : at + count, :] = ref[row_slice(ROWS * i + first, count, step), :]


def relay_kernel(source_ref, target_ref):
    target_ref[...] = source_ref[...]


def merge_phases(parts, lane):
    turned = [parts[0]] + [pltpu.roll(parts[p], 32 * p, 1) for p in (1, 2, 3)]
    quarter = lane // 32
    merged = []
    for k in range(4):
        block = turned[(3 - k) % 4]
        for q in range(3):
            block = jnp.where(quarter == q, turned[(q - k) % 4], block)
        order = 32 * ((lane % 4 + k) % 4) + lane // 4
        merged.append(jnp.take_along_axis(block, order, axis=1))
    return merged


def code_of(scaled):
    whole = jnp.round(scaled)
    r = scaled - whole
    s = r * r
    q = Q_COEFFS[-1]
    for c in Q_COEFFS[-2::-1]:
        q = q * s + c
    return whole + (r * s) * q


def compress_kernel(
    phase_ref, ylow_ref, yhigh_ref, xlow_ref, xhigh_ref, peaks_ref, out_hbm,
    known0, known2, codes0, codes2, full0, full2, fullc0, fullc2, out_ref, sems,
):
    lane = lax.broadcasted_iota(jnp.int32, (8, 128), 1)
    known = (known0, known2)
    codes = (codes0, codes2)
    full = (full0, full2)
    fullc = (fullc0, fullc2)

    def plane(x):
        return (x + OWN_X) * ROWS

    for z in range(2):
        for x in range(16):
            base = plane(x) + OWN_R
            known[z][base : base + 8, :] = phase_ref[2 * z, pl.ds(16 * x, 8, stride=2), :]
    for source, rows, places, shift in ((ylow_ref, LOW_ROWS, LOW_AT, -16), (yhigh_ref, HIGH_ROWS, HIGH_AT, 16)):
        for (z, y, step), at in zip(rows, places):
            r = plane(0) + OWN_R + (y + shift) // 2
            for half in range(2 // step):
                known[z][pl.ds(r + 8 * half * ROWS, 8, stride=step * ROWS), :] = source[at + 8 * half : at + 8 * half + 8, :]
    for source, pieces, shift in ((xlow_ref, LOW_PIECES, -16), (xhigh_ref, HIGH_PIECES, 16)):
        for _, z, x, first, count, step, at in pieces:
            known[z][row_slice(plane(x + shift) + first, count, step), :] = source[at : at + count, :]

    parts = [peaks_ref[8 * i : 8 * i + 8, :] for i in range(peaks_ref.shape[0] // 8)]
    while len(parts) > 1:
        parts = [jnp.maximum(p, q) for p, q in zip(parts[::2], parts[1::2])]
    peaks = parts[0]
    upper = jnp.max(jnp.where(lane < 64, peaks, -jnp.inf))
    lower = jnp.max(jnp.where(lane < 64, -jnp.inf, peaks))
    step = jnp.full((1, 1), 2.0 * (REL_BOUND * (upper + lower)), F32)
    inverse = 1.0 / step

    def quantize(values, outer_low, inner_low, inner_high, outer_high):
        predicted = 0.5625 * (inner_low + inner_high) - 0.0625 * (outer_low + outer_high)
        code = code_of((values - predicted) * inverse)
        return code, predicted + step * code

    for x in range(-2, 19, 4):
        rows = [plane(x + d) + OWN_R - 4 for d in (0, -6, -2, 2, 6)]
        args = [known0[pl.ds(r, 8, stride=2), :] for r in rows]
        code, value = quantize(*args)
        known0[pl.ds(rows[0], 8, stride=2), :] = value
        codes0[pl.ds(rows[0], 8, stride=2), :] = code
    rows = [plane(-2 + d) + OWN_R + 12 for d in (0, -6, -2, 2, 6)]
    args = [known0[pl.ds(r, 6, stride=4 * ROWS), :] for r in rows]
    code, value = quantize(*args)
    known0[pl.ds(rows[0], 6, stride=4 * ROWS), :] = value

    for x in range(-2, 19, 2):
        first = plane(x) + OWN_R - 1
        args = [known0[pl.ds(first + d, 6, stride=2), :] for d in (0, -3, -1, 1, 3)]
        code, value = quantize(*args)
        known0[pl.ds(first, 6, stride=2), :] = value
        codes0[pl.ds(first, 6, stride=2), :] = code

    for x in range(-2, 19, 2):
        for first, count in ((OWN_R - 1, 8), (OWN_R + 7, 3)):
            rows = pl.ds(plane(x) + first, count)
            k = known0[rows, :]
            code, value = quantize(
                known2[rows, :], pltpu.roll(k, 1, 1), k, pltpu.roll(k, 127, 1), pltpu.roll(k, 126, 1)
            )
            known2[rows, :] = value
            codes2[rows, :] = code
    for x in range(0, 16, 4):
        codes0[pl.ds(plane(x) + OWN_R, 4, stride=2), :] = jnp.zeros((4, 128), F32)

    for x in range(1, 16, 2):
        for first, count in ((OWN_R - 1, 8), (OWN_R + 7, 3)):
            for z in range(2):
                args = [known[z][pl.ds(plane(x + d) + first, count), :] for d in (0, -3, -1, 1, 3)]
                code, value = quantize(*args)
                known[z][pl.ds(plane(x) + first, count), :] = value
                codes[z][pl.ds(plane(x) + first, count), :] = code

    def last_steps(x):
        for z in range(2):
            base = plane(x) + OWN_R
            inner = known[z][pl.ds(base, 8), :]
            code, value = quantize(
                phase_ref[2 * z, pl.ds(16 * x + 1, 8, stride=2), :],
                known[z][pl.ds(base - 1, 8), :],
                inner,
                known[z][pl.ds(base + 1, 8), :],
                known[z][pl.ds(base + 2, 8), :],
            )
            full[z][pl.ds(16 * x, 8, stride=2), :] = inner
            full[z][pl.ds(16 * x + 1, 8, stride=2), :] = value
            fullc[z][pl.ds(16 * x, 8, stride=2), :] = codes[z][pl.ds(base, 8), :]
            fullc[z][pl.ds(16 * x + 1, 8, stride=2), :] = code
        for t in range(2):
            rows = slice(16 * x + 8 * t, 16 * x + 8 * t + 8)
            k0 = full0[rows, :]
            k2 = full2[rows, :]
            k0_next = pltpu.roll(k0, 127, 1)
            k2_next = pltpu.roll(k2, 127, 1)
            k2_last = pltpu.roll(k2, 1, 1)
            code1, _ = quantize(phase_ref[1, rows, :], k2_last, k0, k2, k0_next)
            code3, _ = quantize(phase_ref[3, rows, :], k0, k2, k0_next, k2_next)
            merged = merge_phases([fullc0[rows, :], code1, fullc2[rows, :], code3], lane)
            for k in range(4):
                out_ref[x, 8 * t : 8 * t + 8, 128 * k : 128 * k + 128] = merged[k]

    copies = []
    for c in range(CHUNKS):
        for x in range(c * CHUNK_X, c * CHUNK_X + CHUNK_X):
            last_steps(x)
        part = pl.ds(c * CHUNK_X, CHUNK_X)
        copies.append(pltpu.make_async_copy(out_ref.at[part], out_hbm.at[part], sems.at[c]))
        copies[c].start()
    for copy in copies:
        copy.wait()


def shards(snapshot):
    nx = lax.axis_size("gx")
    ny = lax.axis_size("gy")
    vmem = pl.BlockSpec(memory_space=pltpu.VMEM)
    hbm = pl.BlockSpec(memory_space=pltpu.HBM)
    block = snapshot.reshape(snapshot.shape[1:])
    params = pltpu.CompilerParams(vmem_limit_bytes=16 * 1024 * 1024)

    def shape(*dims):
        return jax.ShapeDtypeStruct(dims, F32)

    block = pltpu.with_memory_space_constraint(block, pltpu.HBM)
    raw, peak = pl.pallas_call(
        prepare_kernel,
        in_specs=[hbm],
        out_specs=[vmem, hbm],
        out_shape=[shape(*block.shape), shape(nx * ny, 128)],
        scratch_shapes=[pltpu.VMEM((nx * ny, 128), F32), pltpu.SemaphoreType.DMA((3,))],
        compiler_params=params,
        name="prepare",
    )(block)
    near, far = pl.pallas_call(
        rows_kernel,
        in_specs=[vmem],
        out_specs=[vmem] * 2,
        out_shape=[shape(TOTAL, 128)] * 2,
        scratch_shapes=[
            pltpu.VMEM((2, 16 * 6, 128), F32),
            pltpu.VMEM((TOTAL, 128), F32),
            pltpu.VMEM((TOTAL, 128), F32),
        ],
        compiler_params=params,
        name="rows",
    )(raw)
    phases = pl.pallas_call(
        split_kernel,
        in_specs=[vmem],
        out_specs=vmem,
        out_shape=shape(4, 256, 128),
        compiler_params=params,
        name="split",
    )(raw)

    def shifted(array, axis, d):
        n = lax.axis_size(axis)
        return lax.ppermute(array, axis, [(i, (i + d) % n) for i in range(n)])

    def exchanged(array, axis, odd):
        n = lax.axis_size(axis)
        return lax.ppermute(array, axis, [(i, (i + (1 if i % 2 == odd else -1)) % n) for i in range(n)])

    peaks = lax.all_to_all(peak, AXES, 0, 0, tiled=True)
    yfar = exchanged(far, "gy", 1)
    ynear = exchanged(near, "gy", 0)
    low, high, ylow, yhigh = pl.pallas_call(
        join_kernel,
        in_specs=[vmem] * 3,
        out_specs=[vmem] * 4,
        out_shape=[shape(48, 128)] + [shape(TOTAL, 128)] * 3,
        scratch_shapes=[
            pltpu.VMEM((ROWS * len(LOW_PLANES), 128), F32),
            pltpu.VMEM((ROWS * len(HIGH_PLANES), 128), F32),
        ],
        compiler_params=params,
        name="join",
    )(phases, yfar, ynear)
    xlow = shifted(low, "gx", 1)
    xhigh = shifted(high, "gx", -1)

    xlow = pl.pallas_call(
        relay_kernel,
        in_specs=[vmem],
        out_specs=vmem,
        out_shape=shape(48, 128),
        compiler_params=params,
        cost_estimate=pl.CostEstimate(flops=2 * 10**9, bytes_accessed=10**6, transcendentals=0),
        name="relay",
    )(xlow)
    codes = pl.pallas_call(
        compress_kernel,
        in_specs=[vmem] * 6,
        out_specs=hbm,
        out_shape=shape(*block.shape),
        scratch_shapes=[pltpu.VMEM((PLANES * ROWS, 128), F32)] * 4
        + [pltpu.VMEM((256, 128), F32)] * 4
        + [pltpu.VMEM(block.shape, F32), pltpu.SemaphoreType.DMA((CHUNKS,))],
        compiler_params=params,
        name="compress",
    )(phases, ylow, yhigh, xlow, xhigh, peaks)
    return codes.reshape(snapshot.shape)


def solution(mesh):
    spec = P(None, "gx", "gy", None)
    return jax.shard_map(shards, mesh=mesh, in_specs=(spec,), out_specs=spec, check_vma=False)
```
